1024 devices in a mesh: inner: 16 (over y, z_hi, core), outer: 64 (over x, z_lo).
Axes of the slice: x: 4, y: 4, z: 32 (z_hi: 2, z_lo: 16; z = z_hi * 16 + z_lo), core: 2. Of those that a mesh axis runs over, the one named last changes fastest.
Arguments:
- tokens: bfloat16 [2048, 4096], P('inner'), may hold values from -6 to 6
- weight_codes: bfloat16 [2, 4096, 11008], P(None, 'inner', 'outer'), may hold values from -1 to 1
- block_scales: float32 [2, 2, 11008], P(None, None, 'outer'), may hold values from 0.01 to 0.08
- grad_hidden: bfloat16 [2048, 11008], P('inner', 'outer'), may hold values from -6 to 6
Outputs:
- hidden: bfloat16 [2048, 11008], P('inner', 'outer')
- token_grads: float32 [2048, 4096], P('inner', 'outer')
- weight_grads: float32 [2, 4096, 11008], P(None, 'inner', 'outer')
The draws below stay inside these ranges and needn't reach their ends.
All inputs are finite; a program needn't handle non-finite values.
Results may differ from the reference program's by a relative error of at most 0.015.
Values may be sent and summed in bfloat16 or wider, within the bound.
A program may use at most 64 MiB of HBM per device.

```python
import math
import jax
import jax.numpy as jnp
from jax import lax

D = 4096
HID = 11008
BLOCK = 2048
TOK_DEV = 128
TOKENS = 2048
N_INNER = 16


def shard_levels(key, shape, cuts, smallest, largest):
    level = 1.0
    for position, shards_of in cuts:
        heights = jax.random.uniform(jax.random.fold_in(jax.random.fold_in(key, 6), position), (shards_of,), jnp.float32, smallest / len(cuts), largest / len(cuts))
        level = level * jnp.repeat(jnp.exp(heights), shape[position] // shards_of).reshape((-1,) + (1,) * (len(shape) - 1 - position))
    return level


def normal_values(stream_key, extent, spread, reach, cuts=(), kind=jnp.bfloat16):
    drawn = jax.random.normal(stream_key, extent, jnp.float32) * spread
    if len(cuts) > 0:
        drawn = shard_levels(stream_key, extent, cuts, -0.22, 0.18) * drawn
    return jnp.clip(drawn, min=-reach, max=reach).astype(kind)


def setup_inputs(seed: int = 0) -> dict:
    seeds = jax.random.split(jax.random.key(seed), 5)
    return {
        "tokens": normal_values(seeds[0], (TOKENS, D), 1.0, 6.0, ((0, 16),)),
        "weight_codes": jnp.clip(jax.random.uniform(seeds[1], (2, D, HID), jnp.float32, -1.0, 1.0) * shard_levels(seeds[1], (2, D, HID), ((1, 16), (2, 64)), -0.4, 0.0), -1.0, 1.0).astype(jnp.bfloat16),
        "block_scales": jnp.clip(jnp.exp(math.log(0.08) - 2.0794415 * jax.random.uniform(seeds[2], (2, D // BLOCK, HID), jnp.float32) ** shard_levels(seeds[2], (2, D // BLOCK, HID), ((2, 64),), -0.2, 0.2)), 0.01, 0.08),
        "grad_hidden": normal_values(seeds[3], (TOKENS, HID), 1.0, 6.0, ((0, 16), (1, 64))),
    }


def reference(tokens, weight_codes, block_scales, grad_hidden):
    scale_rows = jnp.repeat(block_scales, BLOCK, axis=1)
    weights = (weight_codes.astype(jnp.float32) * scale_rows).astype(jnp.bfloat16)
    gate = jnp.dot(tokens, weights[0], preferred_element_type=jnp.float32)
    up_proj = jnp.dot(tokens, weights[1], preferred_element_type=jnp.float32)
    sigmoid_gate = jax.nn.sigmoid(gate)
    hidden = (gate * sigmoid_gate * up_proj).astype(jnp.bfloat16)
    cotangent = grad_hidden.astype(jnp.float32)
    d_gate = (cotangent * up_proj * sigmoid_gate * (1.0 + gate * (1.0 - sigmoid_gate))).astype(jnp.bfloat16)
    d_up = (cotangent * gate * sigmoid_gate).astype(jnp.bfloat16)
    token_grads = lax.dot_general(d_gate, weights[0], (((1,), (1,)), ((), ())), preferred_element_type=jnp.float32)
    token_grads = token_grads + lax.dot_general(d_up, weights[1], (((1,), (1,)), ((), ())), preferred_element_type=jnp.float32)
    left_side = jnp.concatenate([d_gate, d_up], axis=1)
    token_blocks = tokens.reshape(N_INNER, TOK_DEV, D)
    factor_blocks = left_side.reshape(N_INNER, TOK_DEV, 2 * HID)

    def advance(running, pair):
        rows, factors = pair
        term = lax.dot_general(rows, factors, (((0,), (0,)), ((), ())), preferred_element_type=jnp.float32)
        rounded = lax.optimization_barrier(term.astype(jnp.bfloat16))
        return (running + rounded.astype(jnp.float32), None)
    running, _ = lax.scan(advance, jnp.zeros((D, 2 * HID), jnp.float32), (token_blocks, factor_blocks))
    weight_grads = running.reshape(D, 2, HID).transpose(1, 0, 2) * (1.0 / math.sqrt(TOKENS))
    return (hidden, token_grads, weight_grads)
```

```python
import math

import jax
import jax.numpy as jnp
from jax import lax
from jax.experimental import pallas as pl
from jax.experimental.pallas import tpu as pltpu
from jax.sharding import PartitionSpec as P

MESH = pl.DeviceIdType.MESH
BLOCK = 2048
F32 = jnp.float32
BF16 = jnp.bfloat16

NY, NX, NA, NB, NZ = 4, 4, 4, 4, 16
HALF = 176
ROWS = 2 * HALF
COLS = 256
TOK = 128
CHUNKS = ((0, 96), (96, 96), (192, 96), (288, 64))
NCH = len(CHUNKS)


def dot(a, b):
    return lax.dot_general(a, b, (((1,), (0,)), ((), ())), preferred_element_type=F32)


def dot_nt(a, b):
    return lax.dot_general(a, b, (((1,), (1,)), ((), ())), preferred_element_type=F32)


def kernel(
    wt_ref, tok_ref, gh_ref, hid_ref, tg_ref, wg_ref,
    w_all, acc, d_t, d_f, d_b,
    x_out, x_in, r_out, r_in, s_out, s_in,
    c_out, c_in, own, y_out, y_in, z_out, z_in,
    fz_s, fz_r, fy_s, fy_r, fc_s, fc_r,
    bc_s, bc_r, by_s, by_r, bz_s, bz_r,
    cx_s, cx_r, cr_s, cr_r, cs_s, cs_r,
):
    me = lax.axis_index("inner")
    ou = lax.axis_index("outer")
    y, zh, c = me // 4, (me // 2) % 2, me % 2
    x, zl = ou // NZ, ou % NZ
    a, b = zl // NB, zl % NB

    def inner(yy, zz, cc):
        return yy * 4 + zz * 2 + cc

    z_dev = {"inner": inner(y, 1 - zh, c)}
    c_dev = {"inner": inner(y, zh, 1 - c)}
    y_dev = [{"inner": inner((y + d) % NY, zh, c)} for d in range(NY)]
    x_dev = [{"outer": ((x + d) % NX) * NZ + zl} for d in range(NX)]
    r_dev = [{"outer": x * NZ + a * NB + (b + d) % NB} for d in range(NB)]
    s_dev = [{"outer": x * NZ + ((a + d) % NA) * NB + b} for d in range(NA)]

    sent = []

    def send(src, dst, s_sem, r_sem, device):
        copy = pltpu.make_async_remote_copy(
            src_ref=src, dst_ref=dst, send_sem=s_sem, recv_sem=r_sem,
            device_id=device, device_id_type=MESH,
        )
        copy.start()
        sent.append(copy)
        return copy

    barrier = pltpu.get_barrier_semaphore()
    peers = [z_dev] + s_dev[1:] + x_dev[1:] + y_dev[1:] + r_dev[1:] + [c_dev]
    for device in peers:
        pl.semaphore_signal(barrier, inc=1, device_id=device, device_id_type=MESH)
    w_all[me] = wt_ref[...]
    acc[...] = jnp.zeros_like(acc)
    pl.semaphore_wait(barrier, len(peers))

    with jax.named_scope("gather_weights"):
        fz, fy, fc = {}, {}, {}
        for k, (at, n) in enumerate(CHUNKS):
            part = w_all.at[me, pl.ds(at, n)]
            fz[k] = send(part, part, fz_s.at[k], fz_r.at[k], z_dev)
        mine = w_all.at[me]
        for d in (1, 3, 2):
            fy[d, 0] = send(mine, mine, fy_s.at[d, 0], fy_r.at[d, 0], y_dev[d])
        fc[0, 0] = send(mine, mine, fc_s.at[0, 0], fc_r.at[0, 0], c_dev)

        def tok_cols(j):
            return tok_ref[:, pl.ds(pl.multiple_of(j * COLS, COLS), COLS)]

        for d in (1, 3, 2):
            fy[d, 0].wait_recv()
            block = w_all.at[inner((y - d + NY) % NY, zh, c)]
            fc[d, 0] = send(block, block, fc_s.at[d, 0], fc_r.at[d, 0], c_dev)
        for d in range(NY):
            fc[d, 0].wait_recv()

        def add_blocks(side, at, n):
            def step(t, _):
                j = inner(t // 2, side, t % 2)
                acc[pl.ds(at, n), :] += dot_nt(w_all[j, pl.ds(at, n), :], tok_cols(j))
                return 0

            lax.fori_loop(0, 2 * NY, step, 0)

        add_blocks(zh, 0, ROWS)

        def pass_on(k):
            at, n = CHUNKS[k]
            for d in (1, 3, 2):
                fy[d, 1 + k].wait_recv()
                part = w_all.at[inner((y - d + NY) % NY, 1 - zh, c), pl.ds(at, n)]
                fc[d, 1 + k] = send(part, part, fc_s.at[d, 1 + k], fc_r.at[d, 1 + k], c_dev)

        def use(k):
            at, n = CHUNKS[k]
            for d in range(NY):
                fc[d, 1 + k].wait_recv()
            add_blocks(1 - zh, at, n)

        for k, (at, n) in enumerate(CHUNKS):
            fz[k].wait_recv()
            part = w_all.at[inner(y, 1 - zh, c), pl.ds(at, n)]
            for d in (1, 3, 2):
                fy[d, 1 + k] = send(part, part, fy_s.at[d, 1 + k], fy_r.at[d, 1 + k], y_dev[d])
            fc[0, 1 + k] = send(part, part, fc_s.at[0, 1 + k], fc_r.at[0, 1 + k], c_dev)
            if k > 0:
                pass_on(k - 1)
                use(k - 1)
        pass_on(NCH - 1)
        use(NCH - 1)

    with jax.named_scope("activations"):
        gate = acc[:HALF, :]
        up = acc[HALF:, :]
        sig = jax.nn.sigmoid(gate)
        silu = gate * sig
        hid_ref[...] = (silu * up).astype(BF16)
        cot = gh_ref[...].astype(F32)
        d_gate = (cot * up * sig * (1.0 + gate * (1.0 - sig))).astype(BF16)
        d_up = (cot * silu).astype(BF16)
        d_t[:HALF, :] = d_gate
        d_t[HALF:, :] = d_up
        d_f[:HALF, :] = d_gate.astype(F32)
        d_f[HALF:ROWS, :] = d_up.astype(F32)
        d_f[ROWS:, :] = jnp.zeros((d_f.shape[0] - ROWS, TOK), F32)
        d_b[...] = d_f[...].T.astype(BF16)

    bc, by, bz = {}, {}, {}

    def weight_part(j):
        return dot(d_t[...], tok_cols(j))

    def to_core(e):
        side = 1 - zh if e == 0 else zh
        for d in (1, 3, 2, 0):
            s = 2 * d + e
            c_out[s] = weight_part(inner((y + d) % NY, side, 1 - c)).astype(BF16)
            bc[s] = send(c_out.at[s], c_in.at[s], bc_s.at[s], bc_r.at[s], c_dev)

    def to_y(e):
        side = 1 - zh if e == 0 else zh
        for d in (1, 3, 2, 0):
            s = 2 * d + e
            part = weight_part(inner((y + d) % NY, side, c))
            bc[s].wait_recv()
            total = part + c_in[s].astype(F32)
            if d == 0:
                own[e] = total
                continue
            y_out[d - 1, e] = total.astype(BF16)
            cuts = CHUNKS if e == 0 else ((0, ROWS),)
            for k, (at, n) in enumerate(cuts):
                slot = k if e == 0 else NCH
                by[d, e, k] = send(
                    y_out.at[d - 1, e, pl.ds(at, n)], y_in.at[d - 1, e, pl.ds(at, n)],
                    by_s.at[d - 1, slot], by_r.at[d - 1, slot], y_dev[d],
                )

    with jax.named_scope("weight_grads_far"):
        to_core(0)
        to_y(0)

    cx, cr, cs = {}, {}, {}
    with jax.named_scope("token_grads_x"):
        for d in (1, 3, 2, 0):
            xb = (x + d) % NX

            def step(q, _, xb=xb):
                x_out[xb, q] = dot(d_b[:, :ROWS], w_all[4 * xb + q]).astype(BF16)
                return 0

            lax.fori_loop(0, 4, step, 0)
            if d > 0:
                cx[d] = send(
                    x_out.at[xb], x_in.at[d - 1], cx_s.at[d - 1], cx_r.at[d - 1], x_dev[d]
                )

    with jax.named_scope("weight_grads_z"):
        for k, (at, n) in enumerate(CHUNKS):
            rows = pl.ds(at, n)
            total = own[0, rows, :]
            for d in (1, 3, 2):
                by[d, 0, k].wait_recv()
                total = total + y_in[d - 1, 0, rows, :].astype(F32)
            z_out[rows, :] = total.astype(BF16)
            bz[k] = send(
                z_out.at[rows], z_in.at[rows], bz_s.at[k], bz_r.at[k], z_dev
            )

    with jax.named_scope("weight_grads_near"):
        to_core(1)
        to_y(1)

    lane = lax.broadcasted_iota(jnp.int32, (TOK, 128), 1)
    low = lane < 64
    with jax.named_scope("token_grads_run"):
        for d in (1, 3, 2):
            cx[d].wait_recv()

        def x_total(q, h):
            cols = pl.ds(128 * h, 128)
            total = x_out[x, q, :, cols].astype(F32)
            for d in (1, 2, 3):
                total = total + x_in[d - 1, q, :, cols].astype(F32)
            return total

        for h in range(2):
            for m in range(2):
                even, odd = x_total(2 * m, h), x_total(2 * m + 1, h)
                r_out[2 * h, m] = jnp.where(low, even, pltpu.roll(odd, 64, 1)).astype(BF16)
                r_out[2 * h + 1, m] = jnp.where(low, pltpu.roll(even, 64, 1), odd).astype(BF16)
        for d in (1, 2, 3):
            cr[d] = send(
                r_out.at[(b + d) % NB], r_in.at[d - 1], cr_s.at[d - 1], cr_r.at[d - 1], r_dev[d]
            )

    with jax.named_scope("weight_grads_own"):
        for d in (1, 3, 2):
            by[d, 1, 0].wait_recv()
        for at, n in CHUNKS:
            rows = pl.ds(at, n)
            total = own[1, rows, :]
            for d in (1, 2, 3):
                total = total + y_in[d - 1, 1, rows, :].astype(F32)
            own[1, rows, :] = total

    with jax.named_scope("token_grads_strided"):
        for d in (1, 2, 3):
            cr[d].wait_recv()
        for m in range(2):
            total = r_out[b, m].astype(F32)
            for d in (1, 2, 3):
                total = total + r_in[d - 1, m].astype(F32)
            turned = pltpu.roll(total, 64, 1)
            s_out[2 * m] = jnp.where(low[:64], total[:64], turned[64:]).astype(BF16)
            s_out[2 * m + 1] = jnp.where(low[:64], turned[:64], total[64:]).astype(BF16)
        for d in (1, 2, 3):
            cs[d] = send(
                s_out.at[(a + d) % NA], s_in.at[d - 1], cs_s.at[d - 1], cs_r.at[d - 1], s_dev[d]
            )
        for d in (1, 2, 3):
            cs[d].wait_recv()
        total = s_out[a].astype(F32)
        for d in (1, 2, 3):
            total = total + s_in[d - 1].astype(F32)
        tg_ref[:64, :] = total[:, :64]
        tg_ref[64:, :] = pltpu.roll(total, 64, 1)[:, :64]

    with jax.named_scope("weight_grads_last"):
        factor = 1.0 / math.sqrt(16 * TOK)
        for k, (at, n) in enumerate(CHUNKS):
            rows = pl.ds(at, n)
            bz[k].wait_recv()
            wg_ref[rows, :] = (own[1, rows, :] + z_in[rows, :].astype(F32)) * factor

    for copy in sent:
        copy.wait_send()


def local(tokens, weight_codes, block_scales, grad_hidden):
    units = weight_codes.shape[2]
    me = lax.axis_index("inner")
    block = me * COLS // BLOCK
    scales = lax.dynamic_index_in_dim(block_scales, block, 1, keepdims=True)
    weights = (weight_codes.astype(F32) * scales).astype(BF16)
    pad = HALF - units
    wt = jnp.pad(weights.transpose(0, 2, 1), ((0, 0), (0, pad), (0, 0))).reshape(ROWS, COLS)
    gh = jnp.pad(grad_hidden.T, ((0, pad), (0, 0)))
    dma = pltpu.SemaphoreType.DMA
    vmem = pl.BlockSpec(memory_space=pltpu.VMEM)
    hidden_t, token_grads, grads_t = pl.pallas_call(
        kernel,
        out_shape=(
            jax.ShapeDtypeStruct((HALF, TOK), BF16),
            jax.ShapeDtypeStruct((TOK, 64), F32),
            jax.ShapeDtypeStruct((ROWS, COLS), F32),
        ),
        in_specs=[vmem] * 3,
        out_specs=(vmem,) * 3,
        scratch_shapes=[
            pltpu.VMEM((16, ROWS, COLS), BF16),
            pltpu.VMEM((ROWS, TOK), F32),
            pltpu.VMEM((ROWS, TOK), BF16),
            pltpu.VMEM((384, TOK), F32),
            pltpu.VMEM((TOK, 384), BF16),
            pltpu.VMEM((NX, 4, TOK, COLS), BF16),
            pltpu.VMEM((NX - 1, 4, TOK, COLS), BF16),
            pltpu.VMEM((NB, 2, TOK, 128), BF16),
            pltpu.VMEM((NB - 1, 2, TOK, 128), BF16),
            pltpu.VMEM((NA, 64, 128), BF16),
            pltpu.VMEM((NA - 1, 64, 128), BF16),
            pltpu.VMEM((8, ROWS, COLS), BF16),
            pltpu.VMEM((8, ROWS, COLS), BF16),
            pltpu.VMEM((2, ROWS, COLS), F32),
            pltpu.VMEM((NY - 1, 2, ROWS, COLS), BF16),
            pltpu.VMEM((NY - 1, 2, ROWS, COLS), BF16),
            pltpu.VMEM((ROWS, COLS), BF16),
            pltpu.VMEM((ROWS, COLS), BF16),
            dma((NCH,)), dma((NCH,)),
            dma((NY, 1 + NCH)), dma((NY, 1 + NCH)),
            dma((NY, 1 + NCH)), dma((NY, 1 + NCH)),
            dma((8,)), dma((8,)),
            dma((NY - 1, 1 + NCH)), dma((NY - 1, 1 + NCH)),
            dma((NCH,)), dma((NCH,)),
            dma((3,)), dma((3,)),
            dma((3,)), dma((3,)),
            dma((3,)), dma((3,)),
        ],
        compiler_params=pltpu.CompilerParams(
            collective_id=0, has_side_effects=True, vmem_limit_bytes=44 * 2**20
        ),
        name="ffn_grads",
    )(wt, tokens, gh)
    hidden = hidden_t[:units].T
    weight_grads = grads_t.reshape(2, HALF, COLS)[:, :units].transpose(0, 2, 1)
    return (hidden, token_grads, weight_grads)


def solution(mesh):
    return jax.shard_map(
        local,
        mesh=mesh,
        in_specs=(
            P("inner", None),
            P(None, "inner", "outer"),
            P(None, None, "outer"),
            P("inner", "outer"),
        ),
        out_specs=(P("inner", "outer"), P("inner", "outer"), P(None, "inner", "outer")),
        check_vma=False,
    )
```

```python
import math

import jax
import jax.numpy as jnp
from jax import lax
from jax.experimental import pallas as pl
from jax.experimental.pallas import tpu as pltpu
from jax.sharding import PartitionSpec as P

MESH = pl.DeviceIdType.MESH
BLOCK = 2048
F32 = jnp.float32
BF16 = jnp.bfloat16

NY, NX, NA, NB, NZ = 4, 4, 4, 4, 16
HALF = 176
ROWS = 2 * HALF
COLS = 256
TOK = 128
CHUNKS = ((0, 96), (96, 96), (192, 96), (288, 64))
NCH = len(CHUNKS)


def dot(a, b):
    return lax.dot_general(a, b, (((1,), (0,)), ((), ())), preferred_element_type=F32)


def dot_nt(a, b):
    return lax.dot_general(a, b, (((1,), (1,)), ((), ())), preferred_element_type=F32)


def kernel(
    wt_ref, tok_ref, gh_ref, hid_ref, tg_ref, wg_ref,
    w_all, acc, d_t, d_f, d_b, d_in, tok_in,
    x_out, x_in, r_out, r_in, s_out, s_in,
    c_out, c_in, own, y_out, y_in,
    fz_s, fz_r, fy_s, fy_r, fc_s, fc_r,
    bz_s, bz_r, bc_s, bc_r, by_s, by_r,
    cx_s, cx_r, cr_s, cr_r, cs_s, cs_r,
    ta_s, ta_r, ts_s, ts_r, tr_s, tr_r, tx_s, tx_r,
):
    me = lax.axis_index("inner")
    ou = lax.axis_index("outer")
    y, zh, c = me // 4, (me // 2) % 2, me % 2
    x, zl = ou // NZ, ou % NZ
    a, b = zl // NB, zl % NB

    def inner(yy, zz, cc):
        return yy * 4 + zz * 2 + cc

    z_dev = {"inner": inner(y, 1 - zh, c)}
    c_dev = {"inner": inner(y, zh, 1 - c)}
    y_dev = [{"inner": inner((y + d) % NY, zh, c)} for d in range(NY)]
    x_dev = [{"outer": ((x + d) % NX) * NZ + zl} for d in range(NX)]
    r_dev = [{"outer": x * NZ + a * NB + (b + d) % NB} for d in range(NB)]
    s_dev = [{"outer": x * NZ + ((a + d) % NA) * NB + b} for d in range(NA)]

    sent = []

    def send(src, dst, s_sem, r_sem, device):
        copy = pltpu.make_async_remote_copy(
            src_ref=src, dst_ref=dst, send_sem=s_sem, recv_sem=r_sem,
            device_id=device, device_id_type=MESH,
        )
        copy.start()
        sent.append(copy)
        return copy

    barrier = pltpu.get_barrier_semaphore()
    peers = [z_dev] + s_dev[1:] + x_dev[1:] + y_dev[1:] + r_dev[1:] + [c_dev]
    for device in peers:
        pl.semaphore_signal(barrier, inc=1, device_id=device, device_id_type=MESH)
    w_all[me] = wt_ref[...]
    acc[...] = jnp.zeros_like(acc)
    pl.semaphore_wait(barrier, len(peers))

    with jax.named_scope("gather_weights"):
        fz, fy, fc = {}, {}, {}
        shard_rows = pl.ds(pl.multiple_of((b % 2) * 64 + a * 16, 16), 16)
        shard = 2 * x + b // 2
        shard_cols = inner(shard // 2, 1 - zh, shard % 2)
        shard_cols = pl.ds(pl.multiple_of(shard_cols * COLS, COLS), COLS)
        ta = send(
            tok_ref.at[shard_rows, shard_cols], tok_in.at[shard, shard_rows],
            ta_s.at[0], ta_r.at[0], z_dev,
        )
        for k, (at, n) in enumerate(CHUNKS):
            part = w_all.at[me, pl.ds(at, n)]
            fz[k] = send(part, part, fz_s.at[k], fz_r.at[k], z_dev)
        mine = w_all.at[me]
        for d in (1, 3, 2):
            fy[d, 0] = send(mine, mine, fy_s.at[d, 0], fy_r.at[d, 0], y_dev[d])
        fc[0, 0] = send(mine, mine, fc_s.at[0, 0], fc_r.at[0, 0], c_dev)

        def tok_cols(j):
            return tok_ref[:, pl.ds(pl.multiple_of(j * COLS, COLS), COLS)]

        for d in (1, 3, 2):
            fy[d, 0].wait_recv()
            block = w_all.at[inner((y - d + NY) % NY, zh, c)]
            fc[d, 0] = send(block, block, fc_s.at[d, 0], fc_r.at[d, 0], c_dev)
        for d in range(NY):
            fc[d, 0].wait_recv()

        def add_blocks(side, at, n):
            def step(t, _):
                j = inner(t // 2, side, t % 2)
                acc[pl.ds(at, n), :] += dot_nt(w_all[j, pl.ds(at, n), :], tok_cols(j))
                return 0

            lax.fori_loop(0, 2 * NY, step, 0)

        add_blocks(zh, 0, ROWS)

        def pass_on(k):
            at, n = CHUNKS[k]
            for d in (1, 3, 2):
                fy[d, 1 + k].wait_recv()
                part = w_all.at[inner((y - d + NY) % NY, 1 - zh, c), pl.ds(at, n)]
                fc[d, 1 + k] = send(part, part, fc_s.at[d, 1 + k], fc_r.at[d, 1 + k], c_dev)

        def use(k):
            at, n = CHUNKS[k]
            for d in range(NY):
                fc[d, 1 + k].wait_recv()
            add_blocks(1 - zh, at, n)

        for k, (at, n) in enumerate(CHUNKS):
            fz[k].wait_recv()
            part = w_all.at[inner(y, 1 - zh, c), pl.ds(at, n)]
            for d in (1, 3, 2):
                fy[d, 1 + k] = send(part, part, fy_s.at[d, 1 + k], fy_r.at[d, 1 + k], y_dev[d])
            fc[0, 1 + k] = send(part, part, fc_s.at[0, 1 + k], fc_r.at[0, 1 + k], c_dev)
            if k > 0:
                pass_on(k - 1)
                use(k - 1)
        ta.wait_recv()
        ts = {}
        for d in (1, 2, 3):
            part = tok_in.at[shard, shard_rows]
            ts[d] = send(part, part, ts_s.at[d - 1], ts_r.at[d - 1], s_dev[d])
        pass_on(NCH - 1)
        use(NCH - 1)

    with jax.named_scope("activations"):
        gate = acc[:HALF, :]
        up = acc[HALF:, :]
        sig = jax.nn.sigmoid(gate)
        silu = gate * sig
        hid_ref[...] = (silu * up).astype(BF16)
        cot = gh_ref[...].astype(F32)
        d_gate = (cot * up * sig * (1.0 + gate * (1.0 - sig))).astype(BF16)
        d_up = (cot * silu).astype(BF16)
        d_t[:HALF, :] = d_gate
        d_t[HALF:, :] = d_up
        bz = {}
        for k, (at, n) in enumerate(CHUNKS):
            rows = pl.ds(at, n)
            bz[k] = send(d_t.at[rows], d_in.at[rows], bz_s.at[k], bz_r.at[k], z_dev)
        d_f[:HALF, :] = d_gate.astype(F32)
        d_f[HALF:ROWS, :] = d_up.astype(F32)
        d_f[ROWS:, :] = jnp.zeros((d_f.shape[0] - ROWS, TOK), F32)
        d_b[...] = d_f[...].T.astype(BF16)

    cx, cr, cs = {}, {}, {}
    with jax.named_scope("token_grads_x"):
        for m in range(2):
            for d in (1, 3, 2, 0):
                xb = (x + d) % NX

                def step(q, _, xb=xb):
                    x_out[xb, q] = dot(d_b[:, :ROWS], w_all[4 * xb + q]).astype(BF16)
                    return 0

                lax.fori_loop(2 * m, 2 * m + 2, step, 0)
                if d > 0:
                    pair = pl.ds(2 * m, 2)
                    cx[d, m] = send(
                        x_out.at[xb, pair], x_in.at[d - 1, pair],
                        cx_s.at[m, d - 1], cx_r.at[m, d - 1], x_dev[d],
                    )

    tr, tx = {}, {}
    with jax.named_scope("tokens_run"):
        for d in (1, 2, 3):
            ts[d].wait_recv()
        run = tok_in.at[shard, pl.ds(pl.multiple_of((b % 2) * 64, 64), 64)]
        for d in (1, 2, 3):
            tr[d] = send(run, run, tr_s.at[d - 1], tr_r.at[d - 1], r_dev[d])

    with jax.named_scope("weight_grads_own_tokens"):

        def step(t, _):
            own[t] = dot(d_t[...], tok_cols(inner(t // 2, zh, t % 2)))
            return 0

        lax.fori_loop(0, 2 * NY, step, 0)

    with jax.named_scope("tokens_x"):
        for d in (1, 2, 3):
            tr[d].wait_recv()
        pair = tok_in.at[pl.ds(2 * x, 2)]
        for d in (1, 3, 2):
            tx[d] = send(pair, pair, tx_s.at[d - 1], tx_r.at[d - 1], x_dev[d])

    lane = lax.broadcasted_iota(jnp.int32, (TOK, 128), 1)
    low = lane < 64

    def x_total(q, h):
        cols = pl.ds(128 * h, 128)
        total = x_out[x, q, :, cols].astype(F32)
        for d in (1, 2, 3):
            total = total + x_in[d - 1, q, :, cols].astype(F32)
        return total

    with jax.named_scope("token_grads_run"):
        for m in range(2):
            for d in (1, 3, 2):
                cx[d, m].wait_recv()
            for h in range(2):
                even, odd = x_total(2 * m, h), x_total(2 * m + 1, h)
                r_out[m, 2 * h] = jnp.where(low, even, pltpu.roll(odd, 64, 1)).astype(BF16)
                r_out[m, 2 * h + 1] = jnp.where(low, pltpu.roll(even, 64, 1), odd).astype(BF16)
            for d in (1, 2, 3):
                cr[d, m] = send(
                    r_out.at[m, (b + d) % NB], r_in.at[m, d - 1],
                    cr_s.at[m, d - 1], cr_r.at[m, d - 1], r_dev[d],
                )

    bc, by = {}, {}
    factor = 1.0 / math.sqrt(16 * TOK)

    def whole(t, rows):
        return own[t, rows, :] + dot(d_in[rows, :], tok_in[t])

    def to_core(k):
        at, n = CHUNKS[k]
        rows = pl.ds(at, n)
        bz[k].wait_recv()
        for yy in range(NY):
            c_out[yy, rows, :] = whole(2 * yy + 1 - c, rows).astype(BF16)
        bc[k] = send(c_out.at[:, rows], c_in.at[:, rows], bc_s.at[k], bc_r.at[k], c_dev)

    def to_y(k):
        at, n = CHUNKS[k]
        rows = pl.ds(at, n)
        bc[k].wait_recv()
        for d in (1, 3, 2, 0):
            yy = (y + d) % NY
            total = whole(2 * yy + c, rows) + c_in[yy, rows, :].astype(F32)
            if d == 0:
                wg_ref[rows, :] = total
                continue
            y_out[d - 1, rows, :] = total.astype(BF16)
            by[d, k] = send(
                y_out.at[d - 1, rows], y_in.at[d - 1, rows],
                by_s.at[k, d - 1], by_r.at[k, d - 1], y_dev[d],
            )

    def finish(k):
        at, n = CHUNKS[k]
        rows = pl.ds(at, n)
        total = wg_ref[rows, :]
        for d in (1, 3, 2):
            by[d, k].wait_recv()
            total = total + y_in[d - 1, rows, :].astype(F32)
        wg_ref[rows, :] = total * factor

    with jax.named_scope("weight_grads_first"):
        for d in (1, 3, 2):
            tx[d].wait_recv()
        to_core(0)
        to_core(1)
        to_y(0)

    with jax.named_scope("token_grads_strided"):
        for m in range(2):
            for d in (1, 2, 3):
                cr[d, m].wait_recv()
            total = r_out[m, b].astype(F32)
            for d in (1, 2, 3):
                total = total + r_in[m, d - 1].astype(F32)
            turned = pltpu.roll(total, 64, 1)
            s_out[2 * m] = jnp.where(low[:64], total[:64], turned[64:]).astype(BF16)
            s_out[2 * m + 1] = jnp.where(low[:64], turned[:64], total[64:]).astype(BF16)
        for d in (1, 2, 3):
            cs[d] = send(
                s_out.at[(a + d) % NA], s_in.at[d - 1], cs_s.at[d - 1], cs_r.at[d - 1], s_dev[d]
            )

    with jax.named_scope("weight_grads_last"):
        to_y(1)
        for k in range(2, NCH):
            to_core(k)
            finish(k - 2)
            to_y(k)
        for k in range(NCH - 2, NCH):
            finish(k)

    with jax.named_scope("token_grads_last"):
        for d in (1, 2, 3):
            cs[d].wait_recv()
        total = s_out[a].astype(F32)
        for d in (1, 2, 3):
            total = total + s_in[d - 1].astype(F32)
        tg_ref[:64, :] = total[:, :64]
        tg_ref[64:, :] = pltpu.roll(total, 64, 1)[:, :64]

    for copy in sent:
        copy.wait_send()


def local(tokens, weight_codes, block_scales, grad_hidden):
    units = weight_codes.shape[2]
    me = lax.axis_index("inner")
    block = me * COLS // BLOCK
    scales = lax.dynamic_index_in_dim(block_scales, block, 1, keepdims=True)
    weights = (weight_codes.astype(F32) * scales).astype(BF16)
    pad = HALF - units
    wt = jnp.pad(weights.transpose(0, 2, 1), ((0, 0), (0, pad), (0, 0))).reshape(ROWS, COLS)
    gh = jnp.pad(grad_hidden.T, ((0, pad), (0, 0)))
    dma = pltpu.SemaphoreType.DMA
    vmem = pl.BlockSpec(memory_space=pltpu.VMEM)
    hidden_t, token_grads, grads_t = pl.pallas_call(
        kernel,
        out_shape=(
            jax.ShapeDtypeStruct((HALF, TOK), BF16),
            jax.ShapeDtypeStruct((TOK, 64), F32),
            jax.ShapeDtypeStruct((ROWS, COLS), F32),
        ),
        in_specs=[vmem] * 3,
        out_specs=(vmem,) * 3,
        scratch_shapes=[
            pltpu.VMEM((16, ROWS, COLS), BF16),
            pltpu.VMEM((ROWS, TOK), F32),
            pltpu.VMEM((ROWS, TOK), BF16),
            pltpu.VMEM((384, TOK), F32),
            pltpu.VMEM((TOK, 384), BF16),
            pltpu.VMEM((ROWS, TOK), BF16),
            pltpu.VMEM((2 * NY, TOK, COLS), BF16),
            pltpu.VMEM((NX, 4, TOK, COLS), BF16),
            pltpu.VMEM((NX - 1, 4, TOK, COLS), BF16),
            pltpu.VMEM((2, NB, TOK, 128), BF16),
            pltpu.VMEM((2, NB - 1, TOK, 128), BF16),
            pltpu.VMEM((NA, 64, 128), BF16),
            pltpu.VMEM((NA - 1, 64, 128), BF16),
            pltpu.VMEM((NY, ROWS, COLS), BF16),
            pltpu.VMEM((NY, ROWS, COLS), BF16),
            pltpu.VMEM((2 * NY, ROWS, COLS), F32),
            pltpu.VMEM((NY - 1, ROWS, COLS), BF16),
            pltpu.VMEM((NY - 1, ROWS, COLS), BF16),
            dma((NCH,)), dma((NCH,)),
            dma((NY, 1 + NCH)), dma((NY, 1 + NCH)),
            dma((NY, 1 + NCH)), dma((NY, 1 + NCH)),
            dma((NCH,)), dma((NCH,)),
            dma((NCH,)), dma((NCH,)),
            dma((NCH, 3)), dma((NCH, 3)),
            dma((2, 3)), dma((2, 3)),
            dma((2, 3)), dma((2, 3)),
            dma((3,)), dma((3,)),
            dma((1,)), dma((1,)),
            dma((3,)), dma((3,)),
            dma((3,)), dma((3,)),
            dma((3,)), dma((3,)),
        ],
        compiler_params=pltpu.CompilerParams(
            collective_id=0, has_side_effects=True, vmem_limit_bytes=44 * 2**20
        ),
        name="ffn_grads",
    )(wt, tokens, gh)
    hidden = hidden_t[:units].T
    weight_grads = grads_t.reshape(2, HALF, COLS)[:, :units].transpose(0, 2, 1)
    return (hidden, token_grads, weight_grads)


def solution(mesh):
    return jax.shard_map(
        local,
        mesh=mesh,
        in_specs=(
            P("inner", None),
            P(None, "inner", "outer"),
            P(None, None, "outer"),
            P("inner", "outer"),
        ),
        out_specs=(P("inner", "outer"), P("inner", "outer"), P(None, "inner", "outer")),
        check_vma=False,
    )
```

```python
import math

import jax
import jax.numpy as jnp
from jax import lax
from jax.experimental import pallas as pl
from jax.experimental.pallas import tpu as pltpu
from jax.sharding import PartitionSpec as P

MESH = pl.DeviceIdType.MESH
BLOCK = 2048
F32 = jnp.float32
BF16 = jnp.bfloat16

NY, NX, NA, NB, NZ = 4, 4, 4, 4, 16
HALF = 176
ROWS = 2 * HALF
COLS = 256
TOK = 128
CHUNKS = ((0, 80), (176, 80), (80, 64), (256, 64), (144, 32), (320, 32))
NCH = len(CHUNKS)
D_CHUNKS = ((0, 96), (96, 96), (192, 96), (288, 64))
NDC = len(D_CHUNKS)


def dot(a, b):
    return lax.dot_general(a, b, (((1,), (0,)), ((), ())), preferred_element_type=F32)


def dot_nt(a, b):
    return lax.dot_general(a, b, (((1,), (1,)), ((), ())), preferred_element_type=F32)


def kernel(
    wt_ref, tok_ref, gh_ref, hid_ref, tg_ref, wg_ref,
    w_all, w_mid, tok_mid, acc, d_t, d_f, d_b, d_in, tok_in,
    x_out, x_in, r_out, r_in, s_out, s_in,
    c_out, c_in, own, y_out, y_in,
    near, f1_s, f1_r, fz_s, fz_r, fy_s, fy_r, fc_s, fc_r,
    bz_s, bz_r, bc_s, bc_r, by_s, by_r,
    cx_s, cx_r, cr_s, cr_r, cs_s, cs_r,
    tm_s, tm_r, ta_s, ta_r, ts_s, ts_r, tr_s, tr_r, tx_s, tx_r,
):
    me = lax.axis_index("inner")
    ou = lax.axis_index("outer")
    y, zh, c = me // 4, (me // 2) % 2, me % 2
    x, zl = ou // NZ, ou % NZ
    a, b = zl // NB, zl % NB

    def inner(yy, zz, cc):
        return yy * 4 + zz * 2 + cc

    z = zh * NZ + zl

    def along(hops):
        far = (z + hops) % (2 * NZ)
        return {"inner": inner(y, far // NZ, c), "outer": x * NZ + far % NZ}

    z_dev = {"inner": inner(y, 1 - zh, c)}
    leg = [along(8), along(24)]
    c_dev = {"inner": inner(y, zh, 1 - c)}
    y_dev = [{"inner": inner((y + d) % NY, zh, c)} for d in range(NY)]
    x_dev = [{"outer": ((x + d) % NX) * NZ + zl} for d in range(NX)]
    r_dev = [{"outer": x * NZ + a * NB + (b + d) % NB} for d in range(NB)]
    s_dev = [{"outer": x * NZ + ((a + d) % NA) * NB + b} for d in range(NA)]

    sent = []

    def send(src, dst, s_sem, r_sem, device):
        copy = pltpu.make_async_remote_copy(
            src_ref=src, dst_ref=dst, send_sem=s_sem, recv_sem=r_sem,
            device_id=device, device_id_type=MESH,
        )
        copy.start()
        sent.append(copy)
        return copy

    barrier = pltpu.get_barrier_semaphore()
    quarter = [along(4), along(28)]
    peers = leg + quarter + x_dev[1:] + y_dev[1:] + r_dev[1:] + [c_dev]
    for device in peers:
        pl.semaphore_signal(barrier, inc=1, device_id=device, device_id_type=MESH)
    w_all[me] = wt_ref[...]
    acc[...] = jnp.zeros_like(acc)
    pl.semaphore_wait(barrier, len(peers))
    for device in quarter:
        pl.semaphore_signal(near, inc=1, device_id=device, device_id_type=MESH)

    with jax.named_scope("gather_weights"):
        f1, fz, fy, fc = {}, {}, {}, {}
        shard = 2 * x + b // 2

        def shard_rows(aa):
            return pl.ds(pl.multiple_of((b % 2) * 64 + aa * 16, 16), 16)

        mine = shard_rows(a)
        shard_cols = inner(shard // 2, 1 - zh, shard % 2)
        shard_cols = pl.ds(pl.multiple_of(shard_cols * COLS, COLS), COLS)
        tok_leg = along(8 + 16 * c)
        tm = send(
            tok_ref.at[mine, shard_cols], tok_mid, tm_s.at[0], tm_r.at[0], tok_leg
        )
        for k, (at, n) in enumerate(CHUNKS):
            part = w_all.at[me, pl.ds(at, n)]
            f1[k] = send(part, w_mid.at[pl.ds(at, n)], f1_s.at[k], f1_r.at[k], leg[k % 2])
        block = w_all.at[me]
        for d in (1, 3, 2):
            fy[d, 0] = send(block, block, fy_s.at[d, 0], fy_r.at[d, 0], y_dev[d])
        fc[0, 0] = send(block, block, fc_s.at[0, 0], fc_r.at[0, 0], c_dev)

        def relay(k):
            at, n = CHUNKS[k]
            f1[k].wait_recv()
            origin = (z + (24 if k % 2 == 0 else 8)) % (2 * NZ) // NZ
            fz[k] = send(
                w_mid.at[pl.ds(at, n)], w_all.at[inner(y, origin, c), pl.ds(at, n)],
                fz_s.at[k], fz_r.at[k], leg[k % 2],
            )

        def tok_cols(j):
            return tok_ref[:, pl.ds(pl.multiple_of(j * COLS, COLS), COLS)]

        def add_blocks(side, at, n):
            total = acc[pl.ds(at, n), :]
            for t in range(2 * NY):
                j = inner(t // 2, side, t % 2)
                total = total + dot_nt(w_all[j, pl.ds(at, n), :], tok_cols(j))
            acc[pl.ds(at, n), :] = total

        def spread(k):
            at, n = CHUNKS[k]
            fz[k].wait_recv()
            part = w_all.at[inner(y, 1 - zh, c), pl.ds(at, n)]
            for d in (1, 3, 2):
                fy[d, 1 + k] = send(part, part, fy_s.at[d, 1 + k], fy_r.at[d, 1 + k], y_dev[d])
            fc[0, 1 + k] = send(part, part, fc_s.at[0, 1 + k], fc_r.at[0, 1 + k], c_dev)

        def pass_on(k):
            at, n = CHUNKS[k]
            for d in (1, 3, 2):
                fy[d, 1 + k].wait_recv()
                part = w_all.at[inner((y - d + NY) % NY, 1 - zh, c), pl.ds(at, n)]
                fc[d, 1 + k] = send(part, part, fc_s.at[d, 1 + k], fc_r.at[d, 1 + k], c_dev)

        def use(k):
            at, n = CHUNKS[k]
            for d in range(NY):
                fc[d, 1 + k].wait_recv()
            add_blocks(1 - zh, at, n)

        tm.wait_recv()
        ta = send(
            tok_mid, tok_in.at[shard, shard_rows((a + 2) % NA)], ta_s.at[0], ta_r.at[0], tok_leg
        )
        relay(0)
        relay(1)
        for d in (1, 3, 2):
            fy[d, 0].wait_recv()
            block = w_all.at[inner((y - d + NY) % NY, zh, c)]
            fc[d, 0] = send(block, block, fc_s.at[d, 0], fc_r.at[d, 0], c_dev)
        relay(2)
        relay(3)
        for d in range(NY):
            fc[d, 0].wait_recv()
        for at in range(0, ROWS, HALF):
            add_blocks(zh, at, HALF)
        spread(0)
        spread(1)
        relay(4)
        relay(5)
        pass_on(0)
        pass_on(1)
        spread(2)
        spread(3)
        use(0)
        use(1)
        pass_on(2)
        pass_on(3)
        spread(4)
        spread(5)
        ta.wait_recv()
        pl.semaphore_wait(near, 2)
        ts = {}
        for d in (1, 2, 3):
            part = tok_in.at[shard, mine]
            ts[d] = send(part, part, ts_s.at[d - 1], ts_r.at[d - 1], s_dev[d])
        use(2)
        use(3)
        pass_on(4)
        pass_on(5)
        use(4)
        use(5)

    with jax.named_scope("activations"):
        gate = acc[:HALF, :]
        up = acc[HALF:, :]
        sig = jax.nn.sigmoid(gate)
        silu = gate * sig
        hid_ref[...] = (silu * up).astype(BF16)
        cot = gh_ref[...].astype(F32)
        d_gate = (cot * up * sig * (1.0 + gate * (1.0 - sig))).astype(BF16)
        d_up = (cot * silu).astype(BF16)
        d_t[:HALF, :] = d_gate
        d_t[HALF:, :] = d_up
        bz = {}
        for k, (at, n) in enumerate(D_CHUNKS):
            rows = pl.ds(at, n)
            bz[k] = send(d_t.at[rows], d_in.at[rows], bz_s.at[k], bz_r.at[k], z_dev)
        d_f[:HALF, :] = d_gate.astype(F32)
        d_f[HALF:ROWS, :] = d_up.astype(F32)
        d_f[ROWS:, :] = jnp.zeros((d_f.shape[0] - ROWS, TOK), F32)
        d_b[...] = d_f[...].T.astype(BF16)

    cx, cr, cs = {}, {}, {}
    with jax.named_scope("token_grads_x"):
        for m in range(2):
            for d in (1, 3, 2, 0):
                xb = (x + d) % NX

                for q in range(2 * m, 2 * m + 2):
                    x_out[xb, q] = dot(d_b[:, :ROWS], w_all[4 * xb + q]).astype(BF16)
                if d > 0:
                    pair = pl.ds(2 * m, 2)
                    cx[d, m] = send(
                        x_out.at[xb, pair], x_in.at[d - 1, pair],
                        cx_s.at[m, d - 1], cx_r.at[m, d - 1], x_dev[d],
                    )

    tr, tx = {}, {}
    with jax.named_scope("tokens_run"):
        for d in (1, 2, 3):
            ts[d].wait_recv()
        run = tok_in.at[shard, pl.ds(pl.multiple_of((b % 2) * 64, 64), 64)]
        for d in (1, 2, 3):
            tr[d] = send(run, run, tr_s.at[d - 1], tr_r.at[d - 1], r_dev[d])

    with jax.named_scope("weight_grads_own_tokens"):

        def step(t, _):
            own[t] = dot(d_t[...], tok_cols(inner(t // 2, zh, t % 2)))
            return 0

        lax.fori_loop(0, 2 * NY, step, 0)

    lane = lax.broadcasted_iota(jnp.int32, (TOK, 128), 1)
    low = lane < 64

    def x_total(q, h):
        cols = pl.ds(128 * h, 128)
        total = x_out[x, q, :, cols].astype(F32)
        for d in (1, 2, 3):
            total = total + x_in[d - 1, q, :, cols].astype(F32)
        return total

    for m in range(2):
        with jax.named_scope("token_grads_run"):
            for d in (1, 3, 2):
                cx[d, m].wait_recv()
            for h in range(2):
                even, odd = x_total(2 * m, h), x_total(2 * m + 1, h)
                r_out[m, 2 * h] = jnp.where(low, even, pltpu.roll(odd, 64, 1)).astype(BF16)
                r_out[m, 2 * h + 1] = jnp.where(low, pltpu.roll(even, 64, 1), odd).astype(BF16)
            for d in (1, 2, 3):
                cr[d, m] = send(
                    r_out.at[m, (b + d) % NB], r_in.at[m, d - 1],
                    cr_s.at[m, d - 1], cr_r.at[m, d - 1], r_dev[d],
                )
        if m == 0:
            with jax.named_scope("tokens_x"):
                for d in (1, 2, 3):
                    tr[d].wait_recv()
                pair = tok_in.at[pl.ds(2 * x, 2)]
                for d in (1, 3, 2):
                    tx[d] = send(pair, pair, tx_s.at[d - 1], tx_r.at[d - 1], x_dev[d])

    bc, by = {}, {}
    factor = 1.0 / math.sqrt(16 * TOK)

    def whole(t, rows):
        return own[t, rows, :] + dot(d_in[rows, :], tok_in[t])

    def to_core(k):
        at, n = D_CHUNKS[k]
        rows = pl.ds(at, n)
        bz[k].wait_recv()
        for yy in range(NY):
            c_out[yy, rows, :] = whole(2 * yy + 1 - c, rows).astype(BF16)
        bc[k] = send(c_out.at[:, rows], c_in.at[:, rows], bc_s.at[k], bc_r.at[k], c_dev)

    def to_y(k):
        at, n = D_CHUNKS[k]
        rows = pl.ds(at, n)
        bc[k].wait_recv()
        for d in (1, 3, 2, 0):
            yy = (y + d) % NY
            total = whole(2 * yy + c, rows) + c_in[yy, rows, :].astype(F32)
            if d == 0:
                wg_ref[rows, :] = total
                continue
            y_out[d - 1, rows, :] = total.astype(BF16)
            by[d, k] = send(
                y_out.at[d - 1, rows], y_in.at[d - 1, rows],
                by_s.at[k, d - 1], by_r.at[k, d - 1], y_dev[d],
            )

    def finish(k):
        at, n = D_CHUNKS[k]
        rows = pl.ds(at, n)
        total = wg_ref[rows, :]
        for d in (1, 3, 2):
            by[d, k].wait_recv()
            total = total + y_in[d - 1, rows, :].astype(F32)
        wg_ref[rows, :] = total * factor

    with jax.named_scope("weight_grads_first"):
        for d in (1, 3, 2):
            tx[d].wait_recv()
        to_core(0)

    with jax.named_scope("token_grads_strided"):
        for m in range(2):
            for d in (1, 2, 3):
                cr[d, m].wait_recv()
            total = r_out[m, b].astype(F32)
            for d in (1, 2, 3):
                total = total + r_in[m, d - 1].astype(F32)
            turned = pltpu.roll(total, 64, 1)
            s_out[2 * m] = jnp.where(low[:64], total[:64], turned[64:]).astype(BF16)
            s_out[2 * m + 1] = jnp.where(low[:64], turned[:64], total[64:]).astype(BF16)
        for d in (1, 2, 3):
            cs[d] = send(
                s_out.at[(a + d) % NA], s_in.at[d - 1], cs_s.at[d - 1], cs_r.at[d - 1], s_dev[d]
            )

    with jax.named_scope("weight_grads_last"):
        to_core(1)
        to_y(0)
        to_y(1)
        for k in range(2, NDC):
            to_core(k)
            finish(k - 2)
            to_y(k)
        for k in range(NDC - 2, NDC):
            finish(k)

    with jax.named_scope("token_grads_last"):
        for d in (1, 2, 3):
            cs[d].wait_recv()
        total = s_out[a].astype(F32)
        for d in (1, 2, 3):
            total = total + s_in[d - 1].astype(F32)
        tg_ref[:64, :] = total[:, :64]
        tg_ref[64:, :] = pltpu.roll(total, 64, 1)[:, :64]

    for copy in sent:
        copy.wait_send()


def local(tokens, weight_codes, block_scales, grad_hidden):
    units = weight_codes.shape[2]
    me = lax.axis_index("inner")
    block = me * COLS // BLOCK
    scales = lax.dynamic_index_in_dim(block_scales, block, 1, keepdims=True)
    weights = (weight_codes.astype(F32) * scales).astype(BF16)
    pad = HALF - units
    wt = jnp.pad(weights.transpose(0, 2, 1), ((0, 0), (0, pad), (0, 0))).reshape(ROWS, COLS)
    gh = jnp.pad(grad_hidden.T, ((0, pad), (0, 0)))
    dma = pltpu.SemaphoreType.DMA
    vmem = pl.BlockSpec(memory_space=pltpu.VMEM)
    hidden_t, token_grads, grads_t = pl.pallas_call(
        kernel,
        out_shape=(
            jax.ShapeDtypeStruct((HALF, TOK), BF16),
            jax.ShapeDtypeStruct((TOK, 64), F32),
            jax.ShapeDtypeStruct((ROWS, COLS), F32),
        ),
        in_specs=[vmem] * 3,
        out_specs=(vmem,) * 3,
        scratch_shapes=[
            pltpu.VMEM((16, ROWS, COLS), BF16),
            pltpu.VMEM((ROWS, COLS), BF16),
            pltpu.VMEM((16, COLS), BF16),
            pltpu.VMEM((ROWS, TOK), F32),
            pltpu.VMEM((ROWS, TOK), BF16),
            pltpu.VMEM((384, TOK), F32),
            pltpu.VMEM((TOK, 384), BF16),
            pltpu.VMEM((ROWS, TOK), BF16),
            pltpu.VMEM((2 * NY, TOK, COLS), BF16),
            pltpu.VMEM((NX, 4, TOK, COLS), BF16),
            pltpu.VMEM((NX - 1, 4, TOK, COLS), BF16),
            pltpu.VMEM((2, NB, TOK, 128), BF16),
            pltpu.VMEM((2, NB - 1, TOK, 128), BF16),
            pltpu.VMEM((NA, 64, 128), BF16),
            pltpu.VMEM((NA - 1, 64, 128), BF16),
            pltpu.VMEM((NY, ROWS, COLS), BF16),
            pltpu.VMEM((NY, ROWS, COLS), BF16),
            pltpu.VMEM((2 * NY, ROWS, COLS), F32),
            pltpu.VMEM((NY - 1, ROWS, COLS), BF16),
            pltpu.VMEM((NY - 1, ROWS, COLS), BF16),
            pltpu.SemaphoreType.REGULAR,
            dma((NCH,)), dma((NCH,)),
            dma((NCH,)), dma((NCH,)),
            dma((NY, 1 + NCH)), dma((NY, 1 + NCH)),
            dma((NY, 1 + NCH)), dma((NY, 1 + NCH)),
            dma((NDC,)), dma((NDC,)),
            dma((NDC,)), dma((NDC,)),
            dma((NDC, 3)), dma((NDC, 3)),
            dma((2, 3)), dma((2, 3)),
            dma((2, 3)), dma((2, 3)),
            dma((3,)), dma((3,)),
            dma((1,)), dma((1,)),
            dma((1,)), dma((1,)),
            dma((3,)), dma((3,)),
            dma((3,)), dma((3,)),
            dma((3,)), dma((3,)),
        ],
        compiler_params=pltpu.CompilerParams(
            collective_id=0, has_side_effects=True, vmem_limit_bytes=44 * 2**20
        ),
        name="ffn_grads",
    )(wt, tokens, gh)
    hidden = hidden_t[:units].T
    weight_grads = grads_t.reshape(2, HALF, COLS)[:, :units].transpose(0, 2, 1)
    return (hidden, token_grads, weight_grads)


def solution(mesh):
    return jax.shard_map(
        local,
        mesh=mesh,
        in_specs=(
            P("inner", None),
            P(None, "inner", "outer"),
            P(None, None, "outer"),
            P("inner", "outer"),
        ),
        out_specs=(P("inner", "outer"), P("inner", "outer"), P(None, "inner", "outer")),
        check_vma=False,
    )
```

```python
import math

import jax
import jax.numpy as jnp
from jax import lax
from jax.experimental import pallas as pl
from jax.experimental.pallas import tpu as pltpu
from jax.sharding import PartitionSpec as P

MESH = pl.DeviceIdType.MESH
BLOCK = 2048
F32 = jnp.float32
BF16 = jnp.bfloat16

NY, NX, NA, NB, NZ = 4, 4, 4, 4, 16
HALF = 176
ROWS = 2 * HALF
COLS = 256
TOK = 128
CHUNKS = ((0, 80), (176, 80), (80, 64), (256, 64), (144, 32), (320, 32))
NCH = len(CHUNKS)


def dot(a, b):
    return lax.dot_general(a, b, (((1,), (0,)), ((), ())), preferred_element_type=F32)


def dot_nt(a, b):
    return lax.dot_general(a, b, (((1,), (1,)), ((), ())), preferred_element_type=F32)


def kernel(
    wt_ref, tok_ref, gh_ref, hid_ref, tg_ref, wg_ref,
    w_all, w_mid, tok_mid, acc, d_t, d_f, d_b, d_in, tok_in,
    x_out, x_mid, x_in, r_out, r_in, s_out, s_in,
    c_out, c_in, own, y_out, y_in,
    near, f1_s, f1_r, fz_s, fz_r, fy_s, fy_r, fc_s, fc_r,
    bz_s, bz_r, bc_s, bc_r, by_s, by_r,
    cm_s, cm_r, cx_s, cx_r, cr_s, cr_r, cs_s, cs_r,
    tm_s, tm_r, ta_s, ta_r, ts_s, ts_r, tr_s, tr_r, tx_s, tx_r,
):
    me = lax.axis_index("inner")
    ou = lax.axis_index("outer")
    y, zh, c = me // 4, (me // 2) % 2, me % 2
    x, zl = ou // NZ, ou % NZ
    a, b = zl // NB, zl % NB

    def inner(yy, zz, cc):
        return yy * 4 + zz * 2 + cc

    z = zh * NZ + zl

    def along(hops):
        far = (z + hops) % (2 * NZ)
        return {"inner": inner(y, far // NZ, c), "outer": x * NZ + far % NZ}

    z_dev = {"inner": inner(y, 1 - zh, c)}
    leg = [along(8), along(24)]
    c_dev = {"inner": inner(y, zh, 1 - c)}
    y_dev = [{"inner": inner((y + d) % NY, zh, c)} for d in range(NY)]
    x_dev = [{"outer": ((x + d) % NX) * NZ + zl} for d in range(NX)]
    r_dev = [{"outer": x * NZ + a * NB + (b + d) % NB} for d in range(NB)]
    s_dev = [{"outer": x * NZ + ((a + d) % NA) * NB + b} for d in range(NA)]

    sent = []

    def send(src, dst, s_sem, r_sem, device):
        copy = pltpu.make_async_remote_copy(
            src_ref=src, dst_ref=dst, send_sem=s_sem, recv_sem=r_sem,
            device_id=device, device_id_type=MESH,
        )
        copy.start()
        sent.append(copy)
        return copy

    barrier = pltpu.get_barrier_semaphore()
    quarter = [along(4), along(28)]
    peers = leg + quarter + x_dev[1:] + y_dev[1:] + r_dev[1:] + [c_dev]
    for device in peers:
        pl.semaphore_signal(barrier, inc=1, device_id=device, device_id_type=MESH)
    w_all[me] = wt_ref[...]
    acc[...] = jnp.zeros_like(acc)
    pl.semaphore_wait(barrier, len(peers))
    for device in quarter:
        pl.semaphore_signal(near, inc=1, device_id=device, device_id_type=MESH)

    with jax.named_scope("gather_weights"):
        f1, fz, fy, fc = {}, {}, {}, {}
        shard = 2 * x + b // 2

        def shard_rows(aa):
            return pl.ds(pl.multiple_of((b % 2) * 64 + aa * 16, 16), 16)

        mine = shard_rows(a)
        shard_cols = inner(shard // 2, 1 - zh, shard % 2)
        shard_cols = pl.ds(pl.multiple_of(shard_cols * COLS, COLS), COLS)
        tok_leg = along(8 + 16 * c)
        tm = send(
            tok_ref.at[mine, shard_cols], tok_mid, tm_s.at[0], tm_r.at[0], tok_leg
        )
        for k, (at, n) in enumerate(CHUNKS):
            part = w_all.at[me, pl.ds(at, n)]
            f1[k] = send(part, w_mid.at[pl.ds(at, n)], f1_s.at[k], f1_r.at[k], leg[k % 2])
        block = w_all.at[me]
        for d in (1, 3, 2):
            fy[d, 0] = send(block, block, fy_s.at[d, 0], fy_r.at[d, 0], y_dev[d])
        fc[0, 0] = send(block, block, fc_s.at[0, 0], fc_r.at[0, 0], c_dev)

        def relay(k):
            at, n = CHUNKS[k]
            f1[k].wait_recv()
            origin = (z + (24 if k % 2 == 0 else 8)) % (2 * NZ) // NZ
            fz[k] = send(
                w_mid.at[pl.ds(at, n)], w_all.at[inner(y, origin, c), pl.ds(at, n)],
                fz_s.at[k], fz_r.at[k], leg[k % 2],
            )

        def tok_cols(j):
            return tok_ref[:, pl.ds(pl.multiple_of(j * COLS, COLS), COLS)]

        def add_blocks(side, at, n):
            total = acc[pl.ds(at, n), :]
            for t in range(2 * NY):
                j = inner(t // 2, side, t % 2)
                total = total + dot_nt(w_all[j, pl.ds(at, n), :], tok_cols(j))
            acc[pl.ds(at, n), :] = total

        def spread(k):
            at, n = CHUNKS[k]
            fz[k].wait_recv()
            part = w_all.at[inner(y, 1 - zh, c), pl.ds(at, n)]
            for d in (1, 3, 2):
                fy[d, 1 + k] = send(part, part, fy_s.at[d, 1 + k], fy_r.at[d, 1 + k], y_dev[d])
            fc[0, 1 + k] = send(part, part, fc_s.at[0, 1 + k], fc_r.at[0, 1 + k], c_dev)

        def pass_on(k):
            at, n = CHUNKS[k]
            for d in (1, 3, 2):
                fy[d, 1 + k].wait_recv()
                part = w_all.at[inner((y - d + NY) % NY, 1 - zh, c), pl.ds(at, n)]
                fc[d, 1 + k] = send(part, part, fc_s.at[d, 1 + k], fc_r.at[d, 1 + k], c_dev)

        def use(k):
            at, n = CHUNKS[k]
            for d in range(NY):
                fc[d, 1 + k].wait_recv()
            add_blocks(1 - zh, at, n)

        tm.wait_recv()
        ta = send(
            tok_mid, tok_in.at[shard, shard_rows((a + 2) % NA)], ta_s.at[0], ta_r.at[0], tok_leg
        )
        relay(0)
        relay(1)
        for d in (1, 3, 2):
            fy[d, 0].wait_recv()
            block = w_all.at[inner((y - d + NY) % NY, zh, c)]
            fc[d, 0] = send(block, block, fc_s.at[d, 0], fc_r.at[d, 0], c_dev)
        relay(2)
        relay(3)
        for d in range(NY):
            fc[d, 0].wait_recv()
        for at in range(0, ROWS, HALF):
            add_blocks(zh, at, HALF)
        spread(0)
        spread(1)
        relay(4)
        relay(5)
        pass_on(0)
        pass_on(1)
        spread(2)
        spread(3)
        ta.wait_recv()
        pl.semaphore_wait(near, 2)
        ts = {}
        for d in (1, 2, 3):
            part = tok_in.at[shard, mine]
            ts[d] = send(part, part, ts_s.at[d - 1], ts_r.at[d - 1], s_dev[d])

    bz = {}

    def activate(p):
        at, n = CHUNKS[2 * p]
        gate_rows, up_rows = pl.ds(at, n), pl.ds(HALF + at, n)
        gate = acc[gate_rows, :]
        up = acc[up_rows, :]
        sig = jax.nn.sigmoid(gate)
        silu = gate * sig
        hid_ref[gate_rows, :] = (silu * up).astype(BF16)
        cot = gh_ref[gate_rows, :].astype(F32)
        d_gate = (cot * up * sig * (1.0 + gate * (1.0 - sig))).astype(BF16)
        d_up = (cot * silu).astype(BF16)
        d_t[gate_rows, :] = d_gate
        d_t[up_rows, :] = d_up
        d_f[gate_rows, :] = d_gate.astype(F32)
        d_f[up_rows, :] = d_up.astype(F32)

    def send_d(p):
        for k in (2 * p, 2 * p + 1):
            rows = pl.ds(*CHUNKS[k])
            bz[k] = send(d_t.at[rows], d_in.at[rows], bz_s.at[k], bz_r.at[k], z_dev)

    with jax.named_scope("activations"):
        use(0)
        use(1)
        pass_on(2)
        pass_on(3)
        activate(0)
        spread(4)
        spread(5)
        send_d(0)
        use(2)
        use(3)
        activate(1)
        send_d(1)
        pass_on(4)
        pass_on(5)
        use(4)
        use(5)
        activate(2)
        send_d(2)
        d_f[ROWS:, :] = jnp.zeros((d_f.shape[0] - ROWS, TOK), F32)
        d_b[...] = d_f[...].T.astype(BF16)

    cm, cx, cr, cs = {}, {}, {}, {}
    tr, tx = {}, {}

    def term(xb, q):
        return dot(d_b[:, :ROWS], w_all[4 * xb + q])

    def send_x(step, q):
        side = 0 if step == 1 else 1
        cx[side, q] = send(
            x_out.at[(x + step) % NX, q], x_in.at[side, q],
            cx_s.at[side, q], cx_r.at[side, q], x_dev[step],
        )

    with jax.named_scope("token_grads_x"):
        for q in range(4):
            xb = (x + 2) % NX
            x_out[xb, q] = term(xb, q).astype(BF16)
            cm[q] = send(
                x_out.at[xb, q], x_mid.at[q], cm_s.at[q], cm_r.at[q], x_dev[1 if q % 2 == 0 else 3]
            )
        for q in range(4):
            step = 3 if q % 2 == 0 else 1
            xb = (x + step) % NX
            x_out[xb, q] = term(xb, q).astype(BF16)
            send_x(step, q)

    with jax.named_scope("tokens_run"):
        for d in (1, 2, 3):
            ts[d].wait_recv()
        run = tok_in.at[shard, pl.ds(pl.multiple_of((b % 2) * 64, 64), 64)]
        for d in (1, 2, 3):
            tr[d] = send(run, run, tr_s.at[d - 1], tr_r.at[d - 1], r_dev[d])

    with jax.named_scope("token_grads_x_sums"):
        for q in range(4):
            step = 1 if q % 2 == 0 else 3
            xb = (x + step) % NX
            part = term(xb, q)
            cm[q].wait_recv()
            x_out[xb, q] = (part + x_mid[q].astype(F32)).astype(BF16)
            send_x(step, q)
        for q in range(4):
            x_out[x, q] = term(x, q).astype(BF16)

    with jax.named_scope("weight_grads_own_tokens"):

        def step(t, _):
            own[t] = dot(d_t[...], tok_cols(inner(t // 2, zh, t % 2)))
            return 0

        lax.fori_loop(0, 2 * NY, step, 0)

    lane = lax.broadcasted_iota(jnp.int32, (TOK, 128), 1)
    low = lane < 64

    def x_total(q, h):
        cols = pl.ds(128 * h, 128)
        total = x_out[x, q, :, cols].astype(F32)
        for side in range(2):
            total = total + x_in[side, q, :, cols].astype(F32)
        return total

    for m in range(2):
        with jax.named_scope("token_grads_run"):
            for q in range(2 * m, 2 * m + 2):
                for side in range(2):
                    cx[side, q].wait_recv()
            for h in range(2):
                even, odd = x_total(2 * m, h), x_total(2 * m + 1, h)
                r_out[m, 2 * h] = jnp.where(low, even, pltpu.roll(odd, 64, 1)).astype(BF16)
                r_out[m, 2 * h + 1] = jnp.where(low, pltpu.roll(even, 64, 1), odd).astype(BF16)
            for d in (1, 2, 3):
                cr[d, m] = send(
                    r_out.at[m, (b + d) % NB], r_in.at[m, d - 1],
                    cr_s.at[m, d - 1], cr_r.at[m, d - 1], r_dev[d],
                )
        if m == 0:
            with jax.named_scope("tokens_x"):
                for d in (1, 2, 3):
                    tr[d].wait_recv()
                pair = tok_in.at[pl.ds(2 * x, 2)]
                for d in (1, 3, 2):
                    tx[d] = send(pair, pair, tx_s.at[d - 1], tx_r.at[d - 1], x_dev[d])

    bc, by = {}, {}
    factor = 1.0 / math.sqrt(16 * TOK)

    def whole(t, rows):
        return own[t, rows, :] + dot(d_in[rows, :], tok_in[t])

    def to_core(k):
        rows = pl.ds(k * HALF, HALF)
        for p in range(k, NCH, 2):
            bz[p].wait_recv()
        for yy in range(NY):
            c_out[yy, rows, :] = whole(2 * yy + 1 - c, rows).astype(BF16)
        bc[k] = send(c_out.at[:, rows], c_in.at[:, rows], bc_s.at[k], bc_r.at[k], c_dev)

    def to_y(k):
        rows = pl.ds(k * HALF, HALF)
        bc[k].wait_recv()
        for d in (1, 3, 2, 0):
            yy = (y + d) % NY
            total = whole(2 * yy + c, rows) + c_in[yy, rows, :].astype(F32)
            if d == 0:
                wg_ref[rows, :] = total
                continue
            y_out[d - 1, rows, :] = total.astype(BF16)
            by[d, k] = send(
                y_out.at[d - 1, rows], y_in.at[d - 1, rows],
                by_s.at[k, d - 1], by_r.at[k, d - 1], y_dev[d],
            )

    def finish(k):
        rows = pl.ds(k * HALF, HALF)
        total = wg_ref[rows, :]
        for d in (1, 3, 2):
            by[d, k].wait_recv()
            total = total + y_in[d - 1, rows, :].astype(F32)
        wg_ref[rows, :] = total * factor

    with jax.named_scope("weight_grads_first"):
        for d in (1, 3, 2):
            tx[d].wait_recv()
        to_core(0)
        to_core(1)

    with jax.named_scope("token_grads_strided"):
        for m in range(2):
            for d in (1, 2, 3):
                cr[d, m].wait_recv()
            total = r_out[m, b].astype(F32)
            for d in (1, 2, 3):
                total = total + r_in[m, d - 1].astype(F32)
            turned = pltpu.roll(total, 64, 1)
            s_out[2 * m] = jnp.where(low[:64], total[:64], turned[64:]).astype(BF16)
            s_out[2 * m + 1] = jnp.where(low[:64], turned[:64], total[64:]).astype(BF16)
        for d in (1, 2, 3):
            cs[d] = send(
                s_out.at[(a + d) % NA], s_in.at[d - 1], cs_s.at[d - 1], cs_r.at[d - 1], s_dev[d]
            )

    with jax.named_scope("weight_grads_last"):
        to_y(0)
        to_y(1)
        finish(0)
        finish(1)

    with jax.named_scope("token_grads_last"):
        for d in (1, 2, 3):
            cs[d].wait_recv()
        total = s_out[a].astype(F32)
        for d in (1, 2, 3):
            total = total + s_in[d - 1].astype(F32)
        tg_ref[:64, :] = total[:, :64]
        tg_ref[64:, :] = pltpu.roll(total, 64, 1)[:, :64]

    for copy in sent:
        copy.wait_send()


def local(tokens, weight_codes, block_scales, grad_hidden):
    units = weight_codes.shape[2]
    me = lax.axis_index("inner")
    block = me * COLS // BLOCK
    scales = lax.dynamic_index_in_dim(block_scales, block, 1, keepdims=True)
    weights = (weight_codes.astype(F32) * scales).astype(BF16)
    pad = HALF - units
    wt = jnp.pad(weights.transpose(0, 2, 1), ((0, 0), (0, pad), (0, 0))).reshape(ROWS, COLS)
    gh = jnp.pad(grad_hidden.T, ((0, pad), (0, 0)))
    dma = pltpu.SemaphoreType.DMA
    vmem = pl.BlockSpec(memory_space=pltpu.VMEM)
    hidden_t, token_grads, grads_t = pl.pallas_call(
        kernel,
        out_shape=(
            jax.ShapeDtypeStruct((HALF, TOK), BF16),
            jax.ShapeDtypeStruct((TOK, 64), F32),
            jax.ShapeDtypeStruct((ROWS, COLS), F32),
        ),
        in_specs=[vmem] * 3,
        out_specs=(vmem,) * 3,
        scratch_shapes=[
            pltpu.VMEM((16, ROWS, COLS), BF16),
            pltpu.VMEM((ROWS, COLS), BF16),
            pltpu.VMEM((16, COLS), BF16),
            pltpu.VMEM((ROWS, TOK), F32),
            pltpu.VMEM((ROWS, TOK), BF16),
            pltpu.VMEM((384, TOK), F32),
            pltpu.VMEM((TOK, 384), BF16),
            pltpu.VMEM((ROWS, TOK), BF16),
            pltpu.VMEM((2 * NY, TOK, COLS), BF16),
            pltpu.VMEM((NX, 4, TOK, COLS), BF16),
            pltpu.VMEM((4, TOK, COLS), BF16),
            pltpu.VMEM((2, 4, TOK, COLS), BF16),
            pltpu.VMEM((2, NB, TOK, 128), BF16),
            pltpu.VMEM((2, NB - 1, TOK, 128), BF16),
            pltpu.VMEM((NA, 64, 128), BF16),
            pltpu.VMEM((NA - 1, 64, 128), BF16),
            pltpu.VMEM((NY, ROWS, COLS), BF16),
            pltpu.VMEM((NY, ROWS, COLS), BF16),
            pltpu.VMEM((2 * NY, ROWS, COLS), F32),
            pltpu.VMEM((NY - 1, ROWS, COLS), BF16),
            pltpu.VMEM((NY - 1, ROWS, COLS), BF16),
            pltpu.SemaphoreType.REGULAR,
            dma((NCH,)), dma((NCH,)),
            dma((NCH,)), dma((NCH,)),
            dma((NY, 1 + NCH)), dma((NY, 1 + NCH)),
            dma((NY, 1 + NCH)), dma((NY, 1 + NCH)),
            dma((NCH,)), dma((NCH,)),
            dma((2,)), dma((2,)),
            dma((2, 3)), dma((2, 3)),
            dma((4,)), dma((4,)),
            dma((2, 4)), dma((2, 4)),
            dma((2, 3)), dma((2, 3)),
            dma((3,)), dma((3,)),
            dma((1,)), dma((1,)),
            dma((1,)), dma((1,)),
            dma((3,)), dma((3,)),
            dma((3,)), dma((3,)),
            dma((3,)), dma((3,)),
        ],
        compiler_params=pltpu.CompilerParams(
            collective_id=0, has_side_effects=True, vmem_limit_bytes=44 * 2**20
        ),
        name="ffn_grads",
    )(wt, tokens, gh)
    hidden = hidden_t[:units].T
    weight_grads = grads_t.reshape(2, HALF, COLS)[:, :units].transpose(0, 2, 1)
    return (hidden, token_grads, weight_grads)


def solution(mesh):
    return jax.shard_map(
        local,
        mesh=mesh,
        in_specs=(
            P("inner", None),
            P(None, "inner", "outer"),
            P(None, None, "outer"),
            P("inner", "outer"),
        ),
        out_specs=(P("inner", "outer"), P("inner", "outer"), P(None, "inner", "outer")),
        check_vma=False,
    )
```

```python
import math

import jax
import jax.numpy as jnp
from jax import lax
from jax.experimental import pallas as pl
from jax.experimental.pallas import tpu as pltpu
from jax.sharding import PartitionSpec as P

MESH = pl.DeviceIdType.MESH
BLOCK = 2048
F32 = jnp.float32
BF16 = jnp.bfloat16

NY, NX, NA, NB, NZ = 4, 4, 4, 4, 16
HALF = 176
ROWS = 2 * HALF
COLS = 256
TOK = 128
CHUNKS = ((0, 80), (176, 80), (80, 64), (256, 64), (144, 32), (320, 32))
NCH = len(CHUNKS)


def dot(a, b):
    return lax.dot_general(a, b, (((1,), (0,)), ((), ())), preferred_element_type=F32)


def dot_nt(a, b):
    return lax.dot_general(a, b, (((1,), (1,)), ((), ())), preferred_element_type=F32)


def kernel(
    wt_ref, tok_ref, gh_ref, hid_ref, tg_ref, wg_ref,
    w_all, w_mid, tok_mid, acc, d_t, d_f, d_b, d_in, tok_in,
    x_out, x_mid, x_in, r_out, r_in, s_own, s_out, s_in,
    c_out, c_in, own, y_out, y_in,
    near, f1_s, f1_r, fz_s, fz_r, fy_s, fy_r, fc_s, fc_r,
    bz_s, bz_r, bc_s, bc_r, by_s, by_r,
    cm_s, cm_r, cx_s, cx_r, cr_s, cr_r, cs_s, cs_r,
    tm_s, tm_r, ta_s, ta_r, ts_s, ts_r, tr_s, tr_r, tx_s, tx_r,
):
    me = lax.axis_index("inner")
    ou = lax.axis_index("outer")
    y, zh, c = me // 4, (me // 2) % 2, me % 2
    x, zl = ou // NZ, ou % NZ
    a, b = zl // NB, zl % NB

    def inner(yy, zz, cc):
        return yy * 4 + zz * 2 + cc

    z = zh * NZ + zl

    def along(hops):
        far = (z + hops) % (2 * NZ)
        return {"inner": inner(y, far // NZ, c), "outer": x * NZ + far % NZ}

    z_dev = {"inner": inner(y, 1 - zh, c)}
    leg = [along(8), along(24)]
    c_dev = {"inner": inner(y, zh, 1 - c)}
    y_dev = [{"inner": inner((y + d) % NY, zh, c)} for d in range(NY)]
    x_dev = [{"outer": ((x + d) % NX) * NZ + zl} for d in range(NX)]
    r_dev = [{"outer": x * NZ + a * NB + (b + d) % NB} for d in range(NB)]
    s_dev = [{"outer": x * NZ + ((a + d) % NA) * NB + b} for d in range(NA)]

    sent = []

    def send(src, dst, s_sem, r_sem, device):
        copy = pltpu.make_async_remote_copy(
            src_ref=src, dst_ref=dst, send_sem=s_sem, recv_sem=r_sem,
            device_id=device, device_id_type=MESH,
        )
        copy.start()
        sent.append(copy)
        return copy

    barrier = pltpu.get_barrier_semaphore()
    quarter = [along(4), along(28)]
    peers = leg + quarter + x_dev[1:] + y_dev[1:] + r_dev[1:] + [c_dev]
    for device in peers:
        pl.semaphore_signal(barrier, inc=1, device_id=device, device_id_type=MESH)
    w_all[me] = wt_ref[...]
    acc[...] = jnp.zeros_like(acc)
    pl.semaphore_wait(barrier, len(peers))
    for device in quarter:
        pl.semaphore_signal(near, inc=1, device_id=device, device_id_type=MESH)

    with jax.named_scope("gather_weights"):
        f1, fz, fy, fc = {}, {}, {}, {}
        shard = 2 * x + b // 2

        def shard_rows(aa):
            return pl.ds(pl.multiple_of((b % 2) * 64 + aa * 16, 16), 16)

        mine = shard_rows(a)
        shard_cols = inner(shard // 2, 1 - zh, shard % 2)
        shard_cols = pl.ds(pl.multiple_of(shard_cols * COLS, COLS), COLS)
        tok_leg = along(8 + 16 * c)
        tm = send(
            tok_ref.at[mine, shard_cols], tok_mid, tm_s.at[0], tm_r.at[0], tok_leg
        )
        for k, (at, n) in enumerate(CHUNKS):
            part = w_all.at[me, pl.ds(at, n)]
            f1[k] = send(part, w_mid.at[pl.ds(at, n)], f1_s.at[k], f1_r.at[k], leg[k % 2])
        block = w_all.at[me]
        for d in (1, 3, 2):
            fy[d, 0] = send(block, block, fy_s.at[d, 0], fy_r.at[d, 0], y_dev[d])
        fc[0, 0] = send(block, block, fc_s.at[0, 0], fc_r.at[0, 0], c_dev)

        def relay(k):
            at, n = CHUNKS[k]
            f1[k].wait_recv()
            origin = (z + (24 if k % 2 == 0 else 8)) % (2 * NZ) // NZ
            fz[k] = send(
                w_mid.at[pl.ds(at, n)], w_all.at[inner(y, origin, c), pl.ds(at, n)],
                fz_s.at[k], fz_r.at[k], leg[k % 2],
            )

        def tok_cols(j):
            return tok_ref[:, pl.ds(pl.multiple_of(j * COLS, COLS), COLS)]

        def add_blocks(side, at, n):
            total = acc[pl.ds(at, n), :]
            for t in range(2 * NY):
                j = inner(t // 2, side, t % 2)
                total = total + dot_nt(w_all[j, pl.ds(at, n), :], tok_cols(j))
            acc[pl.ds(at, n), :] = total

        def spread(k):
            at, n = CHUNKS[k]
            fz[k].wait_recv()
            part = w_all.at[inner(y, 1 - zh, c), pl.ds(at, n)]
            for d in (1, 3, 2):
                fy[d, 1 + k] = send(part, part, fy_s.at[d, 1 + k], fy_r.at[d, 1 + k], y_dev[d])
            fc[0, 1 + k] = send(part, part, fc_s.at[0, 1 + k], fc_r.at[0, 1 + k], c_dev)

        def pass_on(k):
            at, n = CHUNKS[k]
            for d in (1, 3, 2):
                fy[d, 1 + k].wait_recv()
                part = w_all.at[inner((y - d + NY) % NY, 1 - zh, c), pl.ds(at, n)]
                fc[d, 1 + k] = send(part, part, fc_s.at[d, 1 + k], fc_r.at[d, 1 + k], c_dev)

        def use(k):
            at, n = CHUNKS[k]
            for d in range(NY):
                fc[d, 1 + k].wait_recv()
            add_blocks(1 - zh, at, n)

        tm.wait_recv()
        ta = send(
            tok_mid, tok_in.at[shard, shard_rows((a + 2) % NA)], ta_s.at[0], ta_r.at[0], tok_leg
        )
        relay(0)
        relay(1)
        for d in (1, 3, 2):
            fy[d, 0].wait_recv()
            block = w_all.at[inner((y - d + NY) % NY, zh, c)]
            fc[d, 0] = send(block, block, fc_s.at[d, 0], fc_r.at[d, 0], c_dev)
        relay(2)
        relay(3)
        for d in range(NY):
            fc[d, 0].wait_recv()
        for at in range(0, ROWS, HALF):
            add_blocks(zh, at, HALF)
        spread(0)
        spread(1)
        relay(4)
        relay(5)
        pass_on(0)
        pass_on(1)
        spread(2)
        spread(3)
        ta.wait_recv()
        pl.semaphore_wait(near, 2)
        ts = {}
        for d in (1, 2, 3):
            part = tok_in.at[shard, mine]
            ts[d] = send(part, part, ts_s.at[d - 1], ts_r.at[d - 1], s_dev[d])

    bz = {}

    def activate(p):
        at, n = CHUNKS[2 * p]
        gate_rows, up_rows = pl.ds(at, n), pl.ds(HALF + at, n)
        gate = acc[gate_rows, :]
        up = acc[up_rows, :]
        sig = jax.nn.sigmoid(gate)
        silu = gate * sig
        hid_ref[gate_rows, :] = (silu * up).astype(BF16)
        cot = gh_ref[gate_rows, :].astype(F32)
        d_gate = (cot * up * sig * (1.0 + gate * (1.0 - sig))).astype(BF16)
        d_up = (cot * silu).astype(BF16)
        d_t[gate_rows, :] = d_gate
        d_t[up_rows, :] = d_up
        d_f[gate_rows, :] = d_gate.astype(F32)
        d_f[up_rows, :] = d_up.astype(F32)

    def send_d(p):
        for k in (2 * p, 2 * p + 1):
            rows = pl.ds(*CHUNKS[k])
            bz[k] = send(d_t.at[rows], d_in.at[rows], bz_s.at[k], bz_r.at[k], z_dev)

    with jax.named_scope("activations"):
        use(0)
        use(1)
        pass_on(2)
        pass_on(3)
        activate(0)
        spread(4)
        spread(5)
        send_d(0)
        use(2)
        use(3)
        activate(1)
        send_d(1)
        pass_on(4)
        pass_on(5)
        use(4)
        use(5)
        activate(2)
        send_d(2)
        tr, tx = {}, {}
        for d in (1, 2, 3):
            ts[d].wait_recv()
        run = tok_in.at[shard, pl.ds(pl.multiple_of((b % 2) * 64, 64), 64)]
        for d in (1, 2, 3):
            tr[d] = send(run, run, tr_s.at[d - 1], tr_r.at[d - 1], r_dev[d])
        d_f[ROWS:, :] = jnp.zeros((d_f.shape[0] - ROWS, TOK), F32)
        d_b[...] = d_f[...].T.astype(BF16)

    cm, cx, cr, cs = {}, {}, {}, {}
    order = (1, 2, 3, 0)
    quarters = [(a + i) % NA for i in range(NA)]

    def term(xb, i):
        return dot(d_b[:, :ROWS], w_all[4 * xb + quarters[i]])

    def send_x(step, i):
        side = 0 if step == 1 else 1
        cx[side, i] = send(
            x_out.at[(x + step) % NX, i], x_in.at[side, i],
            cx_s.at[side, i], cx_r.at[side, i], x_dev[step],
        )

    with jax.named_scope("token_grads_x"):
        for i in order:
            xb = (x + 2) % NX
            x_out[xb, i] = term(xb, i).astype(BF16)
            cm[i] = send(
                x_out.at[xb, i], x_mid.at[i], cm_s.at[i], cm_r.at[i], x_dev[1 if i % 2 == 0 else 3]
            )
        for i in order:
            step = 3 if i % 2 == 0 else 1
            xb = (x + step) % NX
            x_out[xb, i] = term(xb, i).astype(BF16)
            send_x(step, i)
        for i in order:
            step = 1 if i % 2 == 0 else 3
            xb = (x + step) % NX
            part = term(xb, i)
            cm[i].wait_recv()
            x_out[xb, i] = (part + x_mid[i].astype(F32)).astype(BF16)
            send_x(step, i)
        for i in order:
            x_out[x, i] = term(x, i).astype(BF16)

    low = lax.broadcasted_iota(jnp.int32, (64, 128), 1) < 64

    def to_run(i):
        for side in range(2):
            cx[side, i].wait_recv()
        for h in range(2):
            cols = pl.ds(128 * h, 128)
            total = x_out[x, i, :, cols].astype(F32)
            for side in range(2):
                total = total + x_in[side, i, :, cols].astype(F32)
            turned = pltpu.roll(total, 64, 1)
            r_out[i, 2 * h] = jnp.where(low, total[:64], turned[64:]).astype(BF16)
            r_out[i, 2 * h + 1] = jnp.where(low, turned[:64], total[64:]).astype(BF16)
        for d in (1, 2, 3):
            cr[d, i] = send(
                r_out.at[i, (b + d) % NB], r_in.at[i, d - 1],
                cr_s.at[i, d - 1], cr_r.at[i, d - 1], r_dev[d],
            )

    def run_total(i):
        for d in (1, 2, 3):
            cr[d, i].wait_recv()
        total = r_out[i, b].astype(F32)
        for d in (1, 2, 3):
            total = total + r_in[i, d - 1].astype(F32)
        return total

    def to_strided(i):
        s_out[i - 1] = run_total(i).astype(BF16)
        cs[i] = send(s_out.at[i - 1], s_in.at[i - 1], cs_s.at[i - 1], cs_r.at[i - 1], s_dev[i])

    def own_tokens(first, last):
        def step(t, _):
            own[t] = dot(d_t[...], tok_cols(inner(t // 2, zh, t % 2)))
            return 0

        lax.fori_loop(first, last, step, 0)

    with jax.named_scope("token_grads_run"):
        to_run(1)
        own_tokens(0, 4)
        to_run(2)
        for d in (1, 2, 3):
            tr[d].wait_recv()
        pair = tok_in.at[pl.ds(2 * x, 2)]
        for d in (1, 3, 2):
            tx[d] = send(pair, pair, tx_s.at[d - 1], tx_r.at[d - 1], x_dev[d])
        to_run(3)
        own_tokens(4, 8)
        to_run(0)
        for i in (1, 2, 3):
            to_strided(i)

    bc, by = {}, {}
    factor = 1.0 / math.sqrt(16 * TOK)

    def whole(t, rows):
        return own[t, rows, :] + dot(d_in[rows, :], tok_in[t])

    def to_core(k):
        rows = pl.ds(k * HALF, HALF)
        for p in range(k, NCH, 2):
            bz[p].wait_recv()
        for yy in range(NY):
            c_out[yy, rows, :] = whole(2 * yy + 1 - c, rows).astype(BF16)
        bc[k] = send(c_out.at[:, rows], c_in.at[:, rows], bc_s.at[k], bc_r.at[k], c_dev)

    def to_y(k):
        rows = pl.ds(k * HALF, HALF)
        bc[k].wait_recv()
        for d in (1, 3, 2, 0):
            yy = (y + d) % NY
            total = whole(2 * yy + c, rows) + c_in[yy, rows, :].astype(F32)
            if d == 0:
                wg_ref[rows, :] = total
                continue
            y_out[d - 1, rows, :] = total.astype(BF16)
            by[d, k] = send(
                y_out.at[d - 1, rows], y_in.at[d - 1, rows],
                by_s.at[k, d - 1], by_r.at[k, d - 1], y_dev[d],
            )

    def finish(k):
        rows = pl.ds(k * HALF, HALF)
        total = wg_ref[rows, :]
        for d in (1, 3, 2):
            by[d, k].wait_recv()
            total = total + y_in[d - 1, rows, :].astype(F32)
        wg_ref[rows, :] = total * factor

    with jax.named_scope("weight_grads_first"):
        for d in (1, 3, 2):
            tx[d].wait_recv()
        to_core(0)
        to_core(1)
        s_own[...] = run_total(0)

    with jax.named_scope("weight_grads_last"):
        to_y(0)
        to_y(1)
        finish(0)
        finish(1)

    with jax.named_scope("token_grads_last"):
        for d in (1, 2, 3):
            cs[d].wait_recv()
        total = s_own[...]
        for i in (1, 2, 3):
            total = total + s_in[i - 1].astype(F32)
        tg_ref[:64, :] = total[:, :64]
        tg_ref[64:, :] = pltpu.roll(total, 64, 1)[:, :64]

    for copy in sent:
        copy.wait_send()


def local(tokens, weight_codes, block_scales, grad_hidden):
    units = weight_codes.shape[2]
    me = lax.axis_index("inner")
    block = me * COLS // BLOCK
    scales = lax.dynamic_index_in_dim(block_scales, block, 1, keepdims=True)
    weights = (weight_codes.astype(F32) * scales).astype(BF16)
    pad = HALF - units
    wt = jnp.pad(weights.transpose(0, 2, 1), ((0, 0), (0, pad), (0, 0))).reshape(ROWS, COLS)
    gh = jnp.pad(grad_hidden.T, ((0, pad), (0, 0)))
    dma = pltpu.SemaphoreType.DMA
    vmem = pl.BlockSpec(memory_space=pltpu.VMEM)
    hidden_t, token_grads, grads_t = pl.pallas_call(
        kernel,
        out_shape=(
            jax.ShapeDtypeStruct((HALF, TOK), BF16),
            jax.ShapeDtypeStruct((TOK, 64), F32),
            jax.ShapeDtypeStruct((ROWS, COLS), F32),
        ),
        in_specs=[vmem] * 3,
        out_specs=(vmem,) * 3,
        scratch_shapes=[
            pltpu.VMEM((16, ROWS, COLS), BF16),
            pltpu.VMEM((ROWS, COLS), BF16),
            pltpu.VMEM((16, COLS), BF16),
            pltpu.VMEM((ROWS, TOK), F32),
            pltpu.VMEM((ROWS, TOK), BF16),
            pltpu.VMEM((384, TOK), F32),
            pltpu.VMEM((TOK, 384), BF16),
            pltpu.VMEM((ROWS, TOK), BF16),
            pltpu.VMEM((2 * NY, TOK, COLS), BF16),
            pltpu.VMEM((NX, 4, TOK, COLS), BF16),
            pltpu.VMEM((4, TOK, COLS), BF16),
            pltpu.VMEM((2, 4, TOK, COLS), BF16),
            pltpu.VMEM((NA, NB, 64, 128), BF16),
            pltpu.VMEM((NA, NB - 1, 64, 128), BF16),
            pltpu.VMEM((64, 128), F32),
            pltpu.VMEM((NA - 1, 64, 128), BF16),
            pltpu.VMEM((NA - 1, 64, 128), BF16),
            pltpu.VMEM((NY, ROWS, COLS), BF16),
            pltpu.VMEM((NY, ROWS, COLS), BF16),
            pltpu.VMEM((2 * NY, ROWS, COLS), F32),
            pltpu.VMEM((NY - 1, ROWS, COLS), BF16),
            pltpu.VMEM((NY - 1, ROWS, COLS), BF16),
            pltpu.SemaphoreType.REGULAR,
            dma((NCH,)), dma((NCH,)),
            dma((NCH,)), dma((NCH,)),
            dma((NY, 1 + NCH)), dma((NY, 1 + NCH)),
            dma((NY, 1 + NCH)), dma((NY, 1 + NCH)),
            dma((NCH,)), dma((NCH,)),
            dma((2,)), dma((2,)),
            dma((2, 3)), dma((2, 3)),
            dma((4,)), dma((4,)),
            dma((2, 4)), dma((2, 4)),
            dma((4, 3)), dma((4, 3)),
            dma((3,)), dma((3,)),
            dma((1,)), dma((1,)),
            dma((1,)), dma((1,)),
            dma((3,)), dma((3,)),
            dma((3,)), dma((3,)),
            dma((3,)), dma((3,)),
        ],
        compiler_params=pltpu.CompilerParams(
            collective_id=0, has_side_effects=True, vmem_limit_bytes=44 * 2**20
        ),
        name="ffn_grads",
    )(wt, tokens, gh)
    hidden = hidden_t[:units].T
    weight_grads = grads_t.reshape(2, HALF, COLS)[:, :units].transpose(0, 2, 1)
    return (hidden, token_grads, weight_grads)


def solution(mesh):
    return jax.shard_map(
        local,
        mesh=mesh,
        in_specs=(
            P("inner", None),
            P(None, "inner", "outer"),
            P(None, None, "outer"),
            P("inner", "outer"),
        ),
        out_specs=(P("inner", "outer"), P("inner", "outer"), P(None, "inner", "outer")),
        check_vma=False,
    )
```

```python
import math

import jax
import jax.numpy as jnp
from jax import lax
from jax.experimental import pallas as pl
from jax.experimental.pallas import tpu as pltpu
from jax.sharding import PartitionSpec as P

MESH = pl.DeviceIdType.MESH
BLOCK = 2048
F32 = jnp.float32
BF16 = jnp.bfloat16

NY, NX, NA, NB, NZ = 4, 4, 4, 4, 16
HALF = 176
ROWS = 2 * HALF
COLS = 256
TOK = 128
CHUNKS = ((0, 80), (176, 80), (80, 64), (256, 64), (144, 32), (320, 32))
NCH = len(CHUNKS)


def dot(a, b):
    return lax.dot_general(a, b, (((1,), (0,)), ((), ())), preferred_element_type=F32)


def dot_nt(a, b):
    return lax.dot_general(a, b, (((1,), (1,)), ((), ())), preferred_element_type=F32)


def kernel(
    wt_ref, tok_ref, gh_ref, hid_ref, tg_ref, wg_ref,
    w_all, w_mid, tok_mid, acc, d_t, d_f, d_b, d_in, tok_in,
    x_out, x_mid, x_in, r_out, r_in, s_own, s_out, s_in,
    tok_peer, d_peer, tok_in_peer, d_in_peer, own, y_out, y_in,
    near, f1_s, f1_r, fz_s, fz_r, fy_s, fy_r, fc_s, fc_r,
    bz_s, bz_r, bt_s, bt_r, bd_s, bd_r, bu_s, bu_r, be_s, be_r, by_s, by_r,
    cm_s, cm_r, cx_s, cx_r, cr_s, cr_r, cs_s, cs_r,
    tm_s, tm_r, ta_s, ta_r, ts_s, ts_r, tr_s, tr_r, tx_s, tx_r,
):
    me = lax.axis_index("inner")
    ou = lax.axis_index("outer")
    y, zh, c = me // 4, (me // 2) % 2, me % 2
    x, zl = ou // NZ, ou % NZ
    a, b = zl // NB, zl % NB

    def inner(yy, zz, cc):
        return yy * 4 + zz * 2 + cc

    z = zh * NZ + zl

    def along(hops):
        far = (z + hops) % (2 * NZ)
        return {"inner": inner(y, far // NZ, c), "outer": x * NZ + far % NZ}

    z_dev = {"inner": inner(y, 1 - zh, c)}
    leg = [along(8), along(24)]
    c_dev = {"inner": inner(y, zh, 1 - c)}
    y_dev = [{"inner": inner((y + d) % NY, zh, c)} for d in range(NY)]
    x_dev = [{"outer": ((x + d) % NX) * NZ + zl} for d in range(NX)]
    r_dev = [{"outer": x * NZ + a * NB + (b + d) % NB} for d in range(NB)]
    s_dev = [{"outer": x * NZ + ((a + d) % NA) * NB + b} for d in range(NA)]

    sent = []

    def send(src, dst, s_sem, r_sem, device):
        copy = pltpu.make_async_remote_copy(
            src_ref=src, dst_ref=dst, send_sem=s_sem, recv_sem=r_sem,
            device_id=device, device_id_type=MESH,
        )
        copy.start()
        sent.append(copy)
        return copy

    barrier = pltpu.get_barrier_semaphore()
    quarter = [along(4), along(28)]
    peers = leg + quarter + x_dev[1:] + y_dev[1:] + r_dev[1:] + [c_dev]
    for device in peers:
        pl.semaphore_signal(barrier, inc=1, device_id=device, device_id_type=MESH)
    w_all[me] = wt_ref[...]
    acc[...] = jnp.zeros_like(acc)
    pl.semaphore_wait(barrier, len(peers))
    for device in quarter:
        pl.semaphore_signal(near, inc=1, device_id=device, device_id_type=MESH)

    with jax.named_scope("gather_weights"):
        f1, fz, fy, fc = {}, {}, {}, {}
        shard = 2 * x + b // 2

        def shard_rows(aa):
            return pl.ds(pl.multiple_of((b % 2) * 64 + aa * 16, 16), 16)

        mine = shard_rows(a)
        shard_cols = inner(shard // 2, 1 - zh, shard % 2)
        shard_cols = pl.ds(pl.multiple_of(shard_cols * COLS, COLS), COLS)
        tok_leg = along(8 + 16 * c)
        tm = send(
            tok_ref.at[mine, shard_cols], tok_mid, tm_s.at[0], tm_r.at[0], tok_leg
        )
        for k, (at, n) in enumerate(CHUNKS):
            part = w_all.at[me, pl.ds(at, n)]
            f1[k] = send(part, w_mid.at[pl.ds(at, n)], f1_s.at[k], f1_r.at[k], leg[k % 2])
        block = w_all.at[me]
        for d in (1, 3, 2):
            fy[d, 0] = send(block, block, fy_s.at[d, 0], fy_r.at[d, 0], y_dev[d])
        fc[0, 0] = send(block, block, fc_s.at[0, 0], fc_r.at[0, 0], c_dev)

        def relay(k):
            at, n = CHUNKS[k]
            f1[k].wait_recv()
            origin = (z + (24 if k % 2 == 0 else 8)) % (2 * NZ) // NZ
            fz[k] = send(
                w_mid.at[pl.ds(at, n)], w_all.at[inner(y, origin, c), pl.ds(at, n)],
                fz_s.at[k], fz_r.at[k], leg[k % 2],
            )

        def tok_cols(j):
            return tok_ref[:, pl.ds(pl.multiple_of(j * COLS, COLS), COLS)]

        def add_blocks(side, at, n):
            total = acc[pl.ds(at, n), :]
            for t in range(2 * NY):
                j = inner(t // 2, side, t % 2)
                total = total + dot_nt(w_all[j, pl.ds(at, n), :], tok_cols(j))
            acc[pl.ds(at, n), :] = total

        def spread(k):
            at, n = CHUNKS[k]
            fz[k].wait_recv()
            part = w_all.at[inner(y, 1 - zh, c), pl.ds(at, n)]
            for d in (1, 3, 2):
                fy[d, 1 + k] = send(part, part, fy_s.at[d, 1 + k], fy_r.at[d, 1 + k], y_dev[d])
            fc[0, 1 + k] = send(part, part, fc_s.at[0, 1 + k], fc_r.at[0, 1 + k], c_dev)

        def pass_on(k):
            at, n = CHUNKS[k]
            for d in (1, 3, 2):
                fy[d, 1 + k].wait_recv()
                part = w_all.at[inner((y - d + NY) % NY, 1 - zh, c), pl.ds(at, n)]
                fc[d, 1 + k] = send(part, part, fc_s.at[d, 1 + k], fc_r.at[d, 1 + k], c_dev)

        def use(k):
            at, n = CHUNKS[k]
            for d in range(NY):
                fc[d, 1 + k].wait_recv()
            add_blocks(1 - zh, at, n)

        bt = {}
        for yy in range(NY):
            bt[yy] = send(
                tok_ref.at[:, pl.ds(pl.multiple_of(inner(yy, zh, 1 - c) * COLS, COLS), COLS)],
                tok_peer.at[yy], bt_s.at[yy], bt_r.at[yy], c_dev,
            )
        tm.wait_recv()
        ta = send(
            tok_mid, tok_in.at[shard, shard_rows((a + 2) % NA)], ta_s.at[0], ta_r.at[0], tok_leg
        )
        relay(0)
        relay(1)
        for d in (1, 3, 2):
            fy[d, 0].wait_recv()
            block = w_all.at[inner((y - d + NY) % NY, zh, c)]
            fc[d, 0] = send(block, block, fc_s.at[d, 0], fc_r.at[d, 0], c_dev)
        relay(2)
        relay(3)
        ta.wait_recv()
        pl.semaphore_wait(near, 2)
        ts = {}
        for d in (1, 2, 3):
            part = tok_in.at[shard, mine]
            ts[d] = send(part, part, ts_s.at[d - 1], ts_r.at[d - 1], s_dev[d])
        for d in range(NY):
            fc[d, 0].wait_recv()
        for at in range(0, ROWS, HALF):
            add_blocks(zh, at, HALF)
        spread(0)
        spread(1)
        relay(4)
        relay(5)
        pass_on(0)
        pass_on(1)
        spread(2)
        spread(3)
        tr, tx = {}, {}
        for d in (1, 2, 3):
            ts[d].wait_recv()
        run = tok_in.at[shard, pl.ds(pl.multiple_of((b % 2) * 64, 64), 64)]
        for d in (1, 2, 3):
            tr[d] = send(run, run, tr_s.at[d - 1], tr_r.at[d - 1], r_dev[d])

    bz, bd = {}, {}

    def activate(p):
        at, n = CHUNKS[2 * p]
        gate_rows, up_rows = pl.ds(at, n), pl.ds(HALF + at, n)
        gate = acc[gate_rows, :]
        up = acc[up_rows, :]
        sig = jax.nn.sigmoid(gate)
        silu = gate * sig
        hid_ref[gate_rows, :] = (silu * up).astype(BF16)
        cot = gh_ref[gate_rows, :].astype(F32)
        d_gate = (cot * up * sig * (1.0 + gate * (1.0 - sig))).astype(BF16)
        d_up = (cot * silu).astype(BF16)
        d_t[gate_rows, :] = d_gate
        d_t[up_rows, :] = d_up
        d_f[gate_rows, :] = d_gate.astype(F32)
        d_f[up_rows, :] = d_up.astype(F32)

    def send_d(p):
        for k in (2 * p, 2 * p + 1):
            rows = pl.ds(*CHUNKS[k])
            bz[k] = send(d_t.at[rows], d_in.at[rows], bz_s.at[k], bz_r.at[k], z_dev)
            bd[k] = send(d_t.at[rows], d_peer.at[rows], bd_s.at[k], bd_r.at[k], c_dev)

    with jax.named_scope("activations"):
        use(0)
        use(1)
        pass_on(2)
        pass_on(3)
        activate(0)
        spread(4)
        spread(5)
        send_d(0)
        use(2)
        use(3)
        pass_on(4)
        pass_on(5)
        activate(1)
        send_d(1)
        for d in (1, 2, 3):
            tr[d].wait_recv()
        pair = tok_in.at[pl.ds(2 * x, 2)]
        for d in (1, 3, 2):
            tx[d] = send(pair, pair, tx_s.at[d - 1], tx_r.at[d - 1], x_dev[d])
        use(4)
        use(5)
        activate(2)
        send_d(2)
        d_f[ROWS:, :] = jnp.zeros((d_f.shape[0] - ROWS, TOK), F32)
        d_b[...] = d_f[...].T.astype(BF16)

    cm, cx, cr, cs = {}, {}, {}, {}
    order = (1, 2, 3, 0)
    quarters = [(a + i) % NA for i in range(NA)]

    def term(xb, i):
        return dot(d_b[:, :ROWS], w_all[4 * xb + quarters[i]])

    def send_x(step, i):
        side = 0 if step == 1 else 1
        cx[side, i] = send(
            x_out.at[(x + step) % NX, i], x_in.at[side, i],
            cx_s.at[side, i], cx_r.at[side, i], x_dev[step],
        )

    with jax.named_scope("token_grads_x"):
        for i in order:
            xb = (x + 2) % NX
            x_out[xb, i] = term(xb, i).astype(BF16)
            cm[i] = send(
                x_out.at[xb, i], x_mid.at[i], cm_s.at[i], cm_r.at[i], x_dev[1 if i % 2 == 0 else 3]
            )
        for i in order:
            step = 3 if i % 2 == 0 else 1
            xb = (x + step) % NX
            x_out[xb, i] = term(xb, i).astype(BF16)
            send_x(step, i)
        for i in order:
            step = 1 if i % 2 == 0 else 3
            xb = (x + step) % NX
            part = term(xb, i)
            cm[i].wait_recv()
            x_out[xb, i] = (part + x_mid[i].astype(F32)).astype(BF16)
            send_x(step, i)
        for i in order:
            x_out[x, i] = term(x, i).astype(BF16)

    low = lax.broadcasted_iota(jnp.int32, (64, 128), 1) < 64

    def to_run(i):
        for side in range(2):
            cx[side, i].wait_recv()
        for h in range(2):
            cols = pl.ds(128 * h, 128)
            total = x_out[x, i, :, cols].astype(F32)
            for side in range(2):
                total = total + x_in[side, i, :, cols].astype(F32)
            turned = pltpu.roll(total, 64, 1)
            r_out[i, 2 * h] = jnp.where(low, total[:64], turned[64:]).astype(BF16)
            r_out[i, 2 * h + 1] = jnp.where(low, turned[:64], total[64:]).astype(BF16)
        for d in (1, 2, 3):
            cr[d, i] = send(
                r_out.at[i, (b + d) % NB], r_in.at[i, d - 1],
                cr_s.at[i, d - 1], cr_r.at[i, d - 1], r_dev[d],
            )

    def run_total(i):
        for d in (1, 2, 3):
            cr[d, i].wait_recv()
        total = r_out[i, b].astype(F32)
        for d in (1, 2, 3):
            total = total + r_in[i, d - 1].astype(F32)
        return total

    def to_strided(i):
        s_out[i - 1] = run_total(i).astype(BF16)
        cs[i] = send(s_out.at[i - 1], s_in.at[i - 1], cs_s.at[i - 1], cs_r.at[i - 1], s_dev[i])

    bu, be, by = {}, {}, {}
    factor = 1.0 / math.sqrt(16 * TOK)

    def tokens_to_core():
        for d in (1, 3, 2):
            tx[d].wait_recv()
        for yy in range(NY):
            bu[yy] = send(
                tok_in.at[2 * yy + 1 - c], tok_in_peer.at[yy], bu_s.at[yy], bu_r.at[yy], c_dev
            )

    def d_to_core(p):
        for k in (2 * p, 2 * p + 1):
            rows = pl.ds(*CHUNKS[k])
            bz[k].wait_recv()
            be[k] = send(d_in.at[rows], d_in_peer.at[rows], be_s.at[k], be_r.at[k], c_dev)

    def own_tokens():
        for k in range(NCH):
            bd[k].wait_recv()
        for yy in range(NY):
            bt[yy].wait_recv()

        def step(yy, _):
            own[yy] = dot(d_t[...], tok_cols(inner(yy, zh, c))) + dot(d_peer[...], tok_peer[yy])
            return 0

        lax.fori_loop(0, NY, step, 0)

    def to_y(k):
        at, n = CHUNKS[k]
        rows = pl.ds(at, n)
        be[k].wait_recv()
        for d in (1, 3, 2, 0):
            yy = (y + d) % NY
            total = (
                own[yy, rows, :]
                + dot(d_in[rows, :], tok_in[2 * yy + c])
                + dot(d_in_peer[rows, :], tok_in_peer[yy])
            )
            if d == 0:
                wg_ref[rows, :] = total
                continue
            y_out[d - 1, rows, :] = total.astype(BF16)
            by[d, k] = send(
                y_out.at[d - 1, rows], y_in.at[d - 1, rows],
                by_s.at[k, d - 1], by_r.at[k, d - 1], y_dev[d],
            )

    def finish(k):
        rows = pl.ds(*CHUNKS[k])
        total = wg_ref[rows, :]
        for d in (1, 3, 2):
            by[d, k].wait_recv()
            total = total + y_in[d - 1, rows, :].astype(F32)
        wg_ref[rows, :] = total * factor

    with jax.named_scope("gradients"):
        tokens_to_core()
        d_to_core(0)
        to_run(1)
        own_tokens()
        to_run(2)
        d_to_core(1)
        to_run(3)
        to_run(0)
        for yy in range(NY):
            bu[yy].wait_recv()
        to_y(0)
        to_y(1)
        to_strided(1)
        to_strided(2)
        to_y(2)
        to_y(3)
        to_strided(3)
        d_to_core(2)
        s_own[...] = run_total(0)
        for k in range(4, NCH):
            to_y(k)
        for k in range(NCH):
            finish(k)

    with jax.named_scope("token_grads_last"):
        for d in (1, 2, 3):
            cs[d].wait_recv()
        total = s_own[...]
        for i in (1, 2, 3):
            total = total + s_in[i - 1].astype(F32)
        tg_ref[:64, :] = total[:, :64]
        tg_ref[64:, :] = pltpu.roll(total, 64, 1)[:, :64]

    for copy in sent:
        copy.wait_send()


def local(tokens, weight_codes, block_scales, grad_hidden):
    units = weight_codes.shape[2]
    me = lax.axis_index("inner")
    block = me * COLS // BLOCK
    scales = lax.dynamic_index_in_dim(block_scales, block, 1, keepdims=True)
    weights = (weight_codes.astype(F32) * scales).astype(BF16)
    pad = HALF - units
    wt = jnp.pad(weights.transpose(0, 2, 1), ((0, 0), (0, pad), (0, 0))).reshape(ROWS, COLS)
    gh = jnp.pad(grad_hidden.T, ((0, pad), (0, 0)))
    dma = pltpu.SemaphoreType.DMA
    vmem = pl.BlockSpec(memory_space=pltpu.VMEM)
    hidden_t, token_grads, grads_t = pl.pallas_call(
        kernel,
        out_shape=(
            jax.ShapeDtypeStruct((HALF, TOK), BF16),
            jax.ShapeDtypeStruct((TOK, 64), F32),
            jax.ShapeDtypeStruct((ROWS, COLS), F32),
        ),
        in_specs=[vmem] * 3,
        out_specs=(vmem,) * 3,
        scratch_shapes=[
            pltpu.VMEM((16, ROWS, COLS), BF16),
            pltpu.VMEM((ROWS, COLS), BF16),
            pltpu.VMEM((16, COLS), BF16),
            pltpu.VMEM((ROWS, TOK), F32),
            pltpu.VMEM((ROWS, TOK), BF16),
            pltpu.VMEM((384, TOK), F32),
            pltpu.VMEM((TOK, 384), BF16),
            pltpu.VMEM((ROWS, TOK), BF16),
            pltpu.VMEM((2 * NY, TOK, COLS), BF16),
            pltpu.VMEM((NX, 4, TOK, COLS), BF16),
            pltpu.VMEM((4, TOK, COLS), BF16),
            pltpu.VMEM((2, 4, TOK, COLS), BF16),
            pltpu.VMEM((NA, NB, 64, 128), BF16),
            pltpu.VMEM((NA, NB - 1, 64, 128), BF16),
            pltpu.VMEM((64, 128), F32),
            pltpu.VMEM((NA - 1, 64, 128), BF16),
            pltpu.VMEM((NA - 1, 64, 128), BF16),
            pltpu.VMEM((NY, TOK, COLS), BF16),
            pltpu.VMEM((ROWS, TOK), BF16),
            pltpu.VMEM((NY, TOK, COLS), BF16),
            pltpu.VMEM((ROWS, TOK), BF16),
            pltpu.VMEM((NY, ROWS, COLS), F32),
            pltpu.VMEM((NY - 1, ROWS, COLS), BF16),
            pltpu.VMEM((NY - 1, ROWS, COLS), BF16),
            pltpu.SemaphoreType.REGULAR,
            dma((NCH,)), dma((NCH,)),
            dma((NCH,)), dma((NCH,)),
            dma((NY, 1 + NCH)), dma((NY, 1 + NCH)),
            dma((NY, 1 + NCH)), dma((NY, 1 + NCH)),
            dma((NCH,)), dma((NCH,)),
            dma((NY,)), dma((NY,)),
            dma((NCH,)), dma((NCH,)),
            dma((NY,)), dma((NY,)),
            dma((NCH,)), dma((NCH,)),
            dma((NCH, 3)), dma((NCH, 3)),
            dma((4,)), dma((4,)),
            dma((2, 4)), dma((2, 4)),
            dma((4, 3)), dma((4, 3)),
            dma((3,)), dma((3,)),
            dma((1,)), dma((1,)),
            dma((1,)), dma((1,)),
            dma((3,)), dma((3,)),
            dma((3,)), dma((3,)),
            dma((3,)), dma((3,)),
        ],
        compiler_params=pltpu.CompilerParams(
            collective_id=0, has_side_effects=True, vmem_limit_bytes=44 * 2**20
        ),
        name="ffn_grads",
    )(wt, tokens, gh)
    hidden = hidden_t[:units].T
    weight_grads = grads_t.reshape(2, HALF, COLS)[:, :units].transpose(0, 2, 1)
    return (hidden, token_grads, weight_grads)


def solution(mesh):
    return jax.shard_map(
        local,
        mesh=mesh,
        in_specs=(
            P("inner", None),
            P(None, "inner", "outer"),
            P(None, None, "outer"),
            P("inner", "outer"),
        ),
        out_specs=(P("inner", "outer"), P("inner", "outer"), P(None, "inner", "outer")),
        check_vma=False,
    )
```

```python
import math

import jax
import jax.numpy as jnp
from jax import lax
from jax.experimental import pallas as pl
from jax.experimental.pallas import tpu as pltpu
from jax.sharding import PartitionSpec as P

MESH = pl.DeviceIdType.MESH
BLOCK = 2048
F32 = jnp.float32
BF16 = jnp.bfloat16

NY, NX, NA, NB, NZ = 4, 4, 4, 4, 16
HALF = 176
ROWS = 2 * HALF
COLS = 256
TOK = 128
CHUNKS = ((0, 80), (176, 80), (80, 64), (256, 64), (144, 32), (320, 32))
NCH = len(CHUNKS)


def dot(a, b):
    return lax.dot_general(a, b, (((1,), (0,)), ((), ())), preferred_element_type=F32)


def dot_nt(a, b):
    return lax.dot_general(a, b, (((1,), (1,)), ((), ())), preferred_element_type=F32)


def kernel(
    wt_ref, tok_ref, gh_ref, hid_ref, tg_ref, wg_ref,
    w_all, w_mid, tok_mid, acc, d_t, d_f, d_b, d_in, tok_in,
    x_out, x_mid, x_in, r_out, r_in, s_own, s_out, s_in,
    tok_peer, d_peer, tok_in_peer, d_in_peer, own, y_out, y_in,
    near, f1_s, f1_r, fz_s, fz_r, fy_s, fy_r, fc_s, fc_r,
    bz_s, bz_r, bt_s, bt_r, bd_s, bd_r, bu_s, bu_r, be_s, be_r, by_s, by_r,
    cm_s, cm_r, cx_s, cx_r, cr_s, cr_r, cs_s, cs_r,
    tm_s, tm_r, ta_s, ta_r, ts_s, ts_r, tr_s, tr_r, tx_s, tx_r,
):
    me = lax.axis_index("inner")
    ou = lax.axis_index("outer")
    y, zh, c = me // 4, (me // 2) % 2, me % 2
    x, zl = ou // NZ, ou % NZ
    a, b = zl // NB, zl % NB

    def inner(yy, zz, cc):
        return yy * 4 + zz * 2 + cc

    z = zh * NZ + zl

    def along(hops):
        far = (z + hops) % (2 * NZ)
        return {"inner": inner(y, far // NZ, c), "outer": x * NZ + far % NZ}

    z_dev = {"inner": inner(y, 1 - zh, c)}
    leg = [along(8), along(24)]
    c_dev = {"inner": inner(y, zh, 1 - c)}
    y_dev = [{"inner": inner((y + d) % NY, zh, c)} for d in range(NY)]
    x_dev = [{"outer": ((x + d) % NX) * NZ + zl} for d in range(NX)]
    r_dev = [{"outer": x * NZ + a * NB + (b + d) % NB} for d in range(NB)]
    s_dev = [{"outer": x * NZ + ((a + d) % NA) * NB + b} for d in range(NA)]

    sent = []

    def send(src, dst, s_sem, r_sem, device):
        copy = pltpu.make_async_remote_copy(
            src_ref=src, dst_ref=dst, send_sem=s_sem, recv_sem=r_sem,
            device_id=device, device_id_type=MESH,
        )
        copy.start()
        sent.append(copy)
        return copy

    barrier = pltpu.get_barrier_semaphore()
    quarter = [along(4), along(28)]
    peers = leg + quarter + x_dev[1:] + y_dev[1:] + r_dev[1:] + [c_dev]
    for device in peers:
        pl.semaphore_signal(barrier, inc=1, device_id=device, device_id_type=MESH)
    w_all[me] = wt_ref[...]
    acc[...] = jnp.zeros_like(acc)
    pl.semaphore_wait(barrier, len(peers))
    for device in quarter:
        pl.semaphore_signal(near, inc=1, device_id=device, device_id_type=MESH)

    with jax.named_scope("gather_weights"):
        f1, fz, fy, fc = {}, {}, {}, {}
        shard = 2 * x + b // 2

        def shard_rows(aa):
            return pl.ds(pl.multiple_of((b % 2) * 64 + aa * 16, 16), 16)

        mine = shard_rows(a)
        shard_cols = inner(shard // 2, 1 - zh, shard % 2)
        shard_cols = pl.ds(pl.multiple_of(shard_cols * COLS, COLS), COLS)
        tok_leg = along(8 + 16 * c)
        tm = send(
            tok_ref.at[mine, shard_cols], tok_mid, tm_s.at[0], tm_r.at[0], tok_leg
        )
        for k, (at, n) in enumerate(CHUNKS):
            part = w_all.at[me, pl.ds(at, n)]
            f1[k] = send(part, w_mid.at[pl.ds(at, n)], f1_s.at[k], f1_r.at[k], leg[k % 2])
        block = w_all.at[me]
        for d in (1, 3, 2):
            fy[d, 0] = send(block, block, fy_s.at[d, 0], fy_r.at[d, 0], y_dev[d])
        fc[0, 0] = send(block, block, fc_s.at[0, 0], fc_r.at[0, 0], c_dev)

        def relay(k):
            at, n = CHUNKS[k]
            f1[k].wait_recv()
            origin = (z + (24 if k % 2 == 0 else 8)) % (2 * NZ) // NZ
            fz[k] = send(
                w_mid.at[pl.ds(at, n)], w_all.at[inner(y, origin, c), pl.ds(at, n)],
                fz_s.at[k], fz_r.at[k], leg[k % 2],
            )

        def tok_cols(j):
            return tok_ref[:, pl.ds(pl.multiple_of(j * COLS, COLS), COLS)]

        def add_blocks(side, at, n):
            total = acc[pl.ds(at, n), :]
            for t in range(2 * NY):
                j = inner(t // 2, side, t % 2)
                total = total + dot_nt(w_all[j, pl.ds(at, n), :], tok_cols(j))
            acc[pl.ds(at, n), :] = total

        def spread(k):
            at, n = CHUNKS[k]
            fz[k].wait_recv()
            part = w_all.at[inner(y, 1 - zh, c), pl.ds(at, n)]
            for d in (1, 3, 2):
                fy[d, 1 + k] = send(part, part, fy_s.at[d, 1 + k], fy_r.at[d, 1 + k], y_dev[d])
            fc[0, 1 + k] = send(part, part, fc_s.at[0, 1 + k], fc_r.at[0, 1 + k], c_dev)

        def pass_on(k):
            at, n = CHUNKS[k]
            for d in (1, 3, 2):
                fy[d, 1 + k].wait_recv()
                part = w_all.at[inner((y - d + NY) % NY, 1 - zh, c), pl.ds(at, n)]
                fc[d, 1 + k] = send(part, part, fc_s.at[d, 1 + k], fc_r.at[d, 1 + k], c_dev)

        def use(k):
            at, n = CHUNKS[k]
            for d in range(NY):
                fc[d, 1 + k].wait_recv()
            add_blocks(1 - zh, at, n)

        bt = {}
        for yy in range(NY):
            bt[yy] = send(
                tok_ref.at[:, pl.ds(pl.multiple_of(inner(yy, zh, 1 - c) * COLS, COLS), COLS)],
                tok_peer.at[yy], bt_s.at[yy], bt_r.at[yy], c_dev,
            )
        tm.wait_recv()
        ta = send(
            tok_mid, tok_in.at[shard, shard_rows((a + 2) % NA)], ta_s.at[0], ta_r.at[0], tok_leg
        )
        relay(0)
        relay(1)
        for d in (1, 3, 2):
            fy[d, 0].wait_recv()
            block = w_all.at[inner((y - d + NY) % NY, zh, c)]
            fc[d, 0] = send(block, block, fc_s.at[d, 0], fc_r.at[d, 0], c_dev)
        relay(2)
        relay(3)
        ta.wait_recv()
        pl.semaphore_wait(near, 2)
        ts = {}
        for d in (1, 2, 3):
            part = tok_in.at[shard, mine]
            ts[d] = send(part, part, ts_s.at[d - 1], ts_r.at[d - 1], s_dev[d])
        relay(4)
        relay(5)
        spread(0)
        spread(1)
        for d in range(NY):
            fc[d, 0].wait_recv()
        for at in range(0, ROWS, HALF):
            add_blocks(zh, at, HALF)
        pass_on(0)
        pass_on(1)
        spread(2)
        spread(3)
        tr, tx = {}, {}
        for d in (1, 2, 3):
            ts[d].wait_recv()
        run = tok_in.at[shard, pl.ds(pl.multiple_of((b % 2) * 64, 64), 64)]
        for d in (1, 2, 3):
            tr[d] = send(run, run, tr_s.at[d - 1], tr_r.at[d - 1], r_dev[d])

    bz, bd = {}, {}

    def activate(p):
        at, n = CHUNKS[2 * p]
        gate_rows, up_rows = pl.ds(at, n), pl.ds(HALF + at, n)
        gate = acc[gate_rows, :]
        up = acc[up_rows, :]
        sig = jax.nn.sigmoid(gate)
        silu = gate * sig
        hid_ref[gate_rows, :] = (silu * up).astype(BF16)
        cot = gh_ref[gate_rows, :].astype(F32)
        d_gate = (cot * up * sig * (1.0 + gate * (1.0 - sig))).astype(BF16)
        d_up = (cot * silu).astype(BF16)
        d_t[gate_rows, :] = d_gate
        d_t[up_rows, :] = d_up
        d_f[gate_rows, :] = d_gate.astype(F32)
        d_f[up_rows, :] = d_up.astype(F32)

    def send_d(p):
        for k in (2 * p, 2 * p + 1):
            rows = pl.ds(*CHUNKS[k])
            bz[k] = send(d_t.at[rows], d_in.at[rows], bz_s.at[k], bz_r.at[k], z_dev)
            bd[k] = send(d_t.at[rows], d_peer.at[rows], bd_s.at[k], bd_r.at[k], c_dev)

    with jax.named_scope("activations"):
        use(0)
        use(1)
        pass_on(2)
        pass_on(3)
        activate(0)
        spread(4)
        spread(5)
        send_d(0)
        use(2)
        use(3)
        pass_on(4)
        pass_on(5)
        activate(1)
        send_d(1)
        for d in (1, 2, 3):
            tr[d].wait_recv()
        pair = tok_in.at[pl.ds(2 * x, 2)]
        for d in (1, 3, 2):
            tx[d] = send(pair, pair, tx_s.at[d - 1], tx_r.at[d - 1], x_dev[d])
        use(4)
        use(5)
        activate(2)
        send_d(2)
        d_f[ROWS:, :] = jnp.zeros((d_f.shape[0] - ROWS, TOK), F32)
        d_b[...] = d_f[...].T.astype(BF16)

    cm, cx, cr, cs = {}, {}, {}, {}
    order = (1, 2, 3, 0)
    quarters = [(a + i) % NA for i in range(NA)]

    def term(xb, i):
        return dot(d_b[:, :ROWS], w_all[4 * xb + quarters[i]])

    def send_x(step, i):
        side = 0 if step == 1 else 1
        cx[side, i] = send(
            x_out.at[(x + step) % NX, i], x_in.at[side, i],
            cx_s.at[side, i], cx_r.at[side, i], x_dev[step],
        )

    with jax.named_scope("token_grads_x"):
        for i in order:
            xb = (x + 2) % NX
            x_out[xb, i] = term(xb, i).astype(BF16)
            cm[i] = send(
                x_out.at[xb, i], x_mid.at[i], cm_s.at[i], cm_r.at[i], x_dev[1 if i % 2 == 0 else 3]
            )
        for i in order:
            step = 3 if i % 2 == 0 else 1
            xb = (x + step) % NX
            x_out[xb, i] = term(xb, i).astype(BF16)
            send_x(step, i)
        for i in order:
            step = 1 if i % 2 == 0 else 3
            xb = (x + step) % NX
            part = term(xb, i)
            cm[i].wait_recv()
            x_out[xb, i] = (part + x_mid[i].astype(F32)).astype(BF16)
            send_x(step, i)
        for i in order:
            x_out[x, i] = term(x, i).astype(BF16)

    low = lax.broadcasted_iota(jnp.int32, (64, 128), 1) < 64

    def to_run(i):
        for side in range(2):
            cx[side, i].wait_recv()
        for h in range(2):
            cols = pl.ds(128 * h, 128)
            total = x_out[x, i, :, cols].astype(F32)
            for side in range(2):
                total = total + x_in[side, i, :, cols].astype(F32)
            turned = pltpu.roll(total, 64, 1)
            r_out[i, 2 * h] = jnp.where(low, total[:64], turned[64:]).astype(BF16)
            r_out[i, 2 * h + 1] = jnp.where(low, turned[:64], total[64:]).astype(BF16)
        for d in (1, 2, 3):
            cr[d, i] = send(
                r_out.at[i, (b + d) % NB], r_in.at[i, d - 1],
                cr_s.at[i, d - 1], cr_r.at[i, d - 1], r_dev[d],
            )

    def run_total(i):
        for d in (1, 2, 3):
            cr[d, i].wait_recv()
        total = r_out[i, b].astype(F32)
        for d in (1, 2, 3):
            total = total + r_in[i, d - 1].astype(F32)
        return total

    def to_strided(i):
        s_out[i - 1] = run_total(i).astype(BF16)
        cs[i] = send(s_out.at[i - 1], s_in.at[i - 1], cs_s.at[i - 1], cs_r.at[i - 1], s_dev[i])

    bu, be, by = {}, {}, {}
    factor = 1.0 / math.sqrt(16 * TOK)

    def tokens_to_core():
        for d in (1, 3, 2):
            tx[d].wait_recv()
        for yy in range(NY):
            bu[yy] = send(
                tok_in.at[2 * yy + 1 - c], tok_in_peer.at[yy], bu_s.at[yy], bu_r.at[yy], c_dev
            )

    def d_to_core(p):
        for k in (2 * p, 2 * p + 1):
            rows = pl.ds(*CHUNKS[k])
            bz[k].wait_recv()
            be[k] = send(d_in.at[rows], d_in_peer.at[rows], be_s.at[k], be_r.at[k], c_dev)

    def own_tokens():
        for k in range(NCH):
            bd[k].wait_recv()
        for yy in range(NY):
            bt[yy].wait_recv()

        def step(yy, _):
            own[yy] = dot(d_t[...], tok_cols(inner(yy, zh, c))) + dot(d_peer[...], tok_peer[yy])
            return 0

        lax.fori_loop(0, NY, step, 0)

    def to_y(k):
        at, n = CHUNKS[k]
        rows = pl.ds(at, n)
        be[k].wait_recv()
        for d in (1, 3, 2, 0):
            yy = (y + d) % NY
            total = (
                own[yy, rows, :]
                + dot(d_in[rows, :], tok_in[2 * yy + c])
                + dot(d_in_peer[rows, :], tok_in_peer[yy])
            )
            if d == 0:
                wg_ref[rows, :] = total
                continue
            y_out[d - 1, rows, :] = total.astype(BF16)
            by[d, k] = send(
                y_out.at[d - 1, rows], y_in.at[d - 1, rows],
                by_s.at[k, d - 1], by_r.at[k, d - 1], y_dev[d],
            )

    def finish(k):
        rows = pl.ds(*CHUNKS[k])
        total = wg_ref[rows, :]
        for d in (1, 3, 2):
            by[d, k].wait_recv()
            total = total + y_in[d - 1, rows, :].astype(F32)
        wg_ref[rows, :] = total * factor

    with jax.named_scope("gradients"):
        to_run(1)
        tokens_to_core()
        own_tokens()
        to_run(2)
        d_to_core(0)
        to_run(3)
        to_run(0)
        for yy in range(NY):
            bu[yy].wait_recv()
        to_y(0)
        to_strided(1)
        to_strided(2)
        to_y(1)
        d_to_core(1)
        to_strided(3)
        d_to_core(2)
        to_y(2)
        to_y(3)
        s_own[...] = run_total(0)
        for k in range(4, NCH):
            to_y(k)
        for k in range(NCH):
            finish(k)

    with jax.named_scope("token_grads_last"):
        for d in (1, 2, 3):
            cs[d].wait_recv()
        total = s_own[...]
        for i in (1, 2, 3):
            total = total + s_in[i - 1].astype(F32)
        tg_ref[:64, :] = total[:, :64]
        tg_ref[64:, :] = pltpu.roll(total, 64, 1)[:, :64]

    for copy in sent:
        copy.wait_send()


def local(tokens, weight_codes, block_scales, grad_hidden):
    units = weight_codes.shape[2]
    me = lax.axis_index("inner")
    block = me * COLS // BLOCK
    scales = lax.dynamic_index_in_dim(block_scales, block, 1, keepdims=True)
    weights = (weight_codes.astype(F32) * scales).astype(BF16)
    pad = HALF - units
    wt = jnp.pad(weights.transpose(0, 2, 1), ((0, 0), (0, pad), (0, 0))).reshape(ROWS, COLS)
    gh = jnp.pad(grad_hidden.T, ((0, pad), (0, 0)))
    dma = pltpu.SemaphoreType.DMA
    vmem = pl.BlockSpec(memory_space=pltpu.VMEM)
    hidden_t, token_grads, grads_t = pl.pallas_call(
        kernel,
        out_shape=(
            jax.ShapeDtypeStruct((HALF, TOK), BF16),
            jax.ShapeDtypeStruct((TOK, 64), F32),
            jax.ShapeDtypeStruct((ROWS, COLS), F32),
        ),
        in_specs=[vmem] * 3,
        out_specs=(vmem,) * 3,
        scratch_shapes=[
            pltpu.VMEM((16, ROWS, COLS), BF16),
            pltpu.VMEM((ROWS, COLS), BF16),
            pltpu.VMEM((16, COLS), BF16),
            pltpu.VMEM((ROWS, TOK), F32),
            pltpu.VMEM((ROWS, TOK), BF16),
            pltpu.VMEM((384, TOK), F32),
            pltpu.VMEM((TOK, 384), BF16),
            pltpu.VMEM((ROWS, TOK), BF16),
            pltpu.VMEM((2 * NY, TOK, COLS), BF16),
            pltpu.VMEM((NX, 4, TOK, COLS), BF16),
            pltpu.VMEM((4, TOK, COLS), BF16),
            pltpu.VMEM((2, 4, TOK, COLS), BF16),
            pltpu.VMEM((NA, NB, 64, 128), BF16),
            pltpu.VMEM((NA, NB - 1, 64, 128), BF16),
            pltpu.VMEM((64, 128), F32),
            pltpu.VMEM((NA - 1, 64, 128), BF16),
            pltpu.VMEM((NA - 1, 64, 128), BF16),
            pltpu.VMEM((NY, TOK, COLS), BF16),
            pltpu.VMEM((ROWS, TOK), BF16),
            pltpu.VMEM((NY, TOK, COLS), BF16),
            pltpu.VMEM((ROWS, TOK), BF16),
            pltpu.VMEM((NY, ROWS, COLS), F32),
            pltpu.VMEM((NY - 1, ROWS, COLS), BF16),
            pltpu.VMEM((NY - 1, ROWS, COLS), BF16),
            pltpu.SemaphoreType.REGULAR,
            dma((NCH,)), dma((NCH,)),
            dma((NCH,)), dma((NCH,)),
            dma((NY, 1 + NCH)), dma((NY, 1 + NCH)),
            dma((NY, 1 + NCH)), dma((NY, 1 + NCH)),
            dma((NCH,)), dma((NCH,)),
            dma((NY,)), dma((NY,)),
            dma((NCH,)), dma((NCH,)),
            dma((NY,)), dma((NY,)),
            dma((NCH,)), dma((NCH,)),
            dma((NCH, 3)), dma((NCH, 3)),
            dma((4,)), dma((4,)),
            dma((2, 4)), dma((2, 4)),
            dma((4, 3)), dma((4, 3)),
            dma((3,)), dma((3,)),
            dma((1,)), dma((1,)),
            dma((1,)), dma((1,)),
            dma((3,)), dma((3,)),
            dma((3,)), dma((3,)),
            dma((3,)), dma((3,)),
        ],
        compiler_params=pltpu.CompilerParams(
            collective_id=0, has_side_effects=True, vmem_limit_bytes=44 * 2**20
        ),
        name="ffn_grads",
    )(wt, tokens, gh)
    hidden = hidden_t[:units].T
    weight_grads = grads_t.reshape(2, HALF, COLS)[:, :units].transpose(0, 2, 1)
    return (hidden, token_grads, weight_grads)


def solution(mesh):
    return jax.shard_map(
        local,
        mesh=mesh,
        in_specs=(
            P("inner", None),
            P(None, "inner", "outer"),
            P(None, None, "outer"),
            P("inner", "outer"),
        ),
        out_specs=(P("inner", "outer"), P("inner", "outer"), P(None, "inner", "outer")),
        check_vma=False,
    )
```

```python
import math

import jax
import jax.numpy as jnp
from jax import lax
from jax.experimental import pallas as pl
from jax.experimental.pallas import tpu as pltpu
from jax.sharding import PartitionSpec as P

MESH = pl.DeviceIdType.MESH
BLOCK = 2048
F32 = jnp.float32
BF16 = jnp.bfloat16

NY, NX, NA, NB, NZ = 4, 4, 4, 4, 16
HALF = 176
ROWS = 2 * HALF
COLS = 256
TOK = 128
CHUNKS = ((0, 80), (176, 80), (80, 64), (256, 64), (144, 32), (320, 32))
NCH = len(CHUNKS)


def dot(a, b):
    return lax.dot_general(a, b, (((1,), (0,)), ((), ())), preferred_element_type=F32)


def dot_nt(a, b):
    return lax.dot_general(a, b, (((1,), (1,)), ((), ())), preferred_element_type=F32)


def kernel(
    wt_ref, tok_ref, gh_ref, hid_ref, tg_ref, wg_ref,
    w_all, w_mid, tok_mid, acc, d_t, d_f, d_b, d_in, tok_in,
    x_out, x_mid, x_in, r_out, r_in, s_own, s_out, s_in,
    tok_peer, d_peer, tok_in_peer, d_in_peer, own, y_out, y_in,
    near, f1_s, f1_r, fz_s, fz_r, fy_s, fy_r, fc_s, fc_r,
    bz_s, bz_r, bt_s, bt_r, bd_s, bd_r, bu_s, bu_r, be_s, be_r, by_s, by_r,
    cm_s, cm_r, cx_s, cx_r, cr_s, cr_r, cs_s, cs_r,
    tm_s, tm_r, ta_s, ta_r, ts_s, ts_r, tr_s, tr_r, tx_s, tx_r,
):
    me = lax.axis_index("inner")
    ou = lax.axis_index("outer")
    y, zh, c = me // 4, (me // 2) % 2, me % 2
    x, zl = ou // NZ, ou % NZ
    a, b = zl // NB, zl % NB

    def inner(yy, zz, cc):
        return yy * 4 + zz * 2 + cc

    z = zh * NZ + zl

    def along(hops):
        far = (z + hops) % (2 * NZ)
        return {"inner": inner(y, far // NZ, c), "outer": x * NZ + far % NZ}

    z_dev = {"inner": inner(y, 1 - zh, c)}
    leg = [along(8), along(24)]
    c_dev = {"inner": inner(y, zh, 1 - c)}
    y_dev = [{"inner": inner((y + d) % NY, zh, c)} for d in range(NY)]
    x_dev = [{"outer": ((x + d) % NX) * NZ + zl} for d in range(NX)]
    r_dev = [{"outer": x * NZ + a * NB + (b + d) % NB} for d in range(NB)]
    s_dev = [{"outer": x * NZ + ((a + d) % NA) * NB + b} for d in range(NA)]

    sent = []

    def send(src, dst, s_sem, r_sem, device):
        copy = pltpu.make_async_remote_copy(
            src_ref=src, dst_ref=dst, send_sem=s_sem, recv_sem=r_sem,
            device_id=device, device_id_type=MESH,
        )
        copy.start()
        sent.append(copy)
        return copy

    barrier = pltpu.get_barrier_semaphore()
    quarter = [along(4), along(28)]
    peers = leg + quarter + x_dev[1:] + y_dev[1:] + r_dev[1:] + [c_dev]
    for device in peers:
        pl.semaphore_signal(barrier, inc=1, device_id=device, device_id_type=MESH)
    w_all[me] = wt_ref[...]
    acc[...] = jnp.zeros_like(acc)
    pl.semaphore_wait(barrier, len(peers))
    for device in quarter:
        pl.semaphore_signal(near, inc=1, device_id=device, device_id_type=MESH)

    with jax.named_scope("gather_weights"):
        f1, fz, fy, fc = {}, {}, {}, {}
        shard = 2 * x + b // 2

        def shard_rows(aa):
            return pl.ds(pl.multiple_of((b % 2) * 64 + aa * 16, 16), 16)

        mine = shard_rows(a)
        shard_cols = inner(shard // 2, 1 - zh, shard % 2)
        shard_cols = pl.ds(pl.multiple_of(shard_cols * COLS, COLS), COLS)
        tok_leg = along(8 + 16 * c)
        tm = send(
            tok_ref.at[mine, shard_cols], tok_mid, tm_s.at[0], tm_r.at[0], tok_leg
        )
        for k, (at, n) in enumerate(CHUNKS):
            part = w_all.at[me, pl.ds(at, n)]
            f1[k] = send(part, w_mid.at[pl.ds(at, n)], f1_s.at[k], f1_r.at[k], leg[k % 2])
        block = w_all.at[me]
        for d in (1, 3, 2):
            fy[d, 0] = send(block, block, fy_s.at[d, 0], fy_r.at[d, 0], y_dev[d])
        fc[0, 0] = send(block, block, fc_s.at[0, 0], fc_r.at[0, 0], c_dev)

        def relay(k):
            at, n = CHUNKS[k]
            f1[k].wait_recv()
            origin = (z + (24 if k % 2 == 0 else 8)) % (2 * NZ) // NZ
            fz[k] = send(
                w_mid.at[pl.ds(at, n)], w_all.at[inner(y, origin, c), pl.ds(at, n)],
                fz_s.at[k], fz_r.at[k], leg[k % 2],
            )

        def tok_cols(j):
            return tok_ref[:, pl.ds(pl.multiple_of(j * COLS, COLS), COLS)]

        def add_blocks(side, at, n):
            total = acc[pl.ds(at, n), :]
            for t in range(2 * NY):
                j = inner(t // 2, side, t % 2)
                total = total + dot_nt(w_all[j, pl.ds(at, n), :], tok_cols(j))
            acc[pl.ds(at, n), :] = total

        def spread(k):
            at, n = CHUNKS[k]
            fz[k].wait_recv()
            part = w_all.at[inner(y, 1 - zh, c), pl.ds(at, n)]
            for d in (1, 3, 2):
                fy[d, 1 + k] = send(part, part, fy_s.at[d, 1 + k], fy_r.at[d, 1 + k], y_dev[d])
            fc[0, 1 + k] = send(part, part, fc_s.at[0, 1 + k], fc_r.at[0, 1 + k], c_dev)

        def pass_on(k):
            at, n = CHUNKS[k]
            for d in (1, 3, 2):
                fy[d, 1 + k].wait_recv()
                part = w_all.at[inner((y - d + NY) % NY, 1 - zh, c), pl.ds(at, n)]
                fc[d, 1 + k] = send(part, part, fc_s.at[d, 1 + k], fc_r.at[d, 1 + k], c_dev)

        def use(k):
            at, n = CHUNKS[k]
            for d in range(NY):
                fc[d, 1 + k].wait_recv()
            add_blocks(1 - zh, at, n)

        bt = {}
        for yy in range(NY):
            bt[yy] = send(
                tok_ref.at[:, pl.ds(pl.multiple_of(inner(yy, zh, 1 - c) * COLS, COLS), COLS)],
                tok_peer.at[yy], bt_s.at[yy], bt_r.at[yy], c_dev,
            )
        tm.wait_recv()
        ta = send(
            tok_mid, tok_in.at[shard, shard_rows((a + 2) % NA)], ta_s.at[0], ta_r.at[0], tok_leg
        )
        relay(0)
        relay(1)
        for d in (1, 3, 2):
            fy[d, 0].wait_recv()
            block = w_all.at[inner((y - d + NY) % NY, zh, c)]
            fc[d, 0] = send(block, block, fc_s.at[d, 0], fc_r.at[d, 0], c_dev)
        relay(2)
        relay(3)
        ta.wait_recv()
        pl.semaphore_wait(near, 2)
        ts = {}
        for d in (1, 2, 3):
            part = tok_in.at[shard, mine]
            ts[d] = send(part, part, ts_s.at[d - 1], ts_r.at[d - 1], s_dev[d])
        for d in range(NY):
            fc[d, 0].wait_recv()
        for at in range(0, ROWS, HALF):
            add_blocks(zh, at, HALF)
        spread(0)
        spread(1)
        relay(4)
        relay(5)
        pass_on(0)
        pass_on(1)
        spread(2)
        spread(3)
        tr, tx = {}, {}
        for d in (1, 2, 3):
            ts[d].wait_recv()
        run = tok_in.at[shard, pl.ds(pl.multiple_of((b % 2) * 64, 64), 64)]
        for d in (1, 2, 3):
            tr[d] = send(run, run, tr_s.at[d - 1], tr_r.at[d - 1], r_dev[d])

    bz, bd = {}, {}

    def activate(p):
        at, n = CHUNKS[2 * p]
        gate_rows, up_rows = pl.ds(at, n), pl.ds(HALF + at, n)
        gate = acc[gate_rows, :]
        up = acc[up_rows, :]
        sig = jax.nn.sigmoid(gate)
        silu = gate * sig
        hid_ref[gate_rows, :] = (silu * up).astype(BF16)
        cot = gh_ref[gate_rows, :].astype(F32)
        d_gate = (cot * up * sig * (1.0 + gate * (1.0 - sig))).astype(BF16)
        d_up = (cot * silu).astype(BF16)
        d_t[gate_rows, :] = d_gate
        d_t[up_rows, :] = d_up
        d_f[gate_rows, :] = d_gate.astype(F32)
        d_f[up_rows, :] = d_up.astype(F32)

    def send_d(p):
        for k in (2 * p, 2 * p + 1):
            rows = pl.ds(*CHUNKS[k])
            bz[k] = send(d_t.at[rows], d_in.at[rows], bz_s.at[k], bz_r.at[k], z_dev)
            bd[k] = send(d_t.at[rows], d_peer.at[rows], bd_s.at[k], bd_r.at[k], c_dev)

    with jax.named_scope("activations"):
        use(0)
        use(1)
        pass_on(2)
        pass_on(3)
        activate(0)
        spread(4)
        spread(5)
        send_d(0)
        use(2)
        use(3)
        pass_on(4)
        pass_on(5)
        activate(1)
        send_d(1)
        for d in (1, 2, 3):
            tr[d].wait_recv()
        pair = tok_in.at[pl.ds(2 * x, 2)]
        for d in (1, 3, 2):
            tx[d] = send(pair, pair, tx_s.at[d - 1], tx_r.at[d - 1], x_dev[d])
        use(4)
        use(5)
        activate(2)
        send_d(2)
        d_f[ROWS:, :] = jnp.zeros((d_f.shape[0] - ROWS, TOK), F32)
        d_b[...] = d_f[...].T.astype(BF16)

    cm, cx, cr, cs = {}, {}, {}, {}
    order = (1, 2, 3, 0)
    quarters = [(a + i) % NA for i in range(NA)]

    def term(xb, i):
        return dot(d_b[:, :ROWS], w_all[4 * xb + quarters[i]])

    def send_x(step, i):
        side = 0 if step == 1 else 1
        cx[side, i] = send(
            x_out.at[(x + step) % NX, i], x_in.at[side, i],
            cx_s.at[side, i], cx_r.at[side, i], x_dev[step],
        )

    with jax.named_scope("token_grads_x"):
        for i in order:
            xb = (x + 2) % NX
            x_out[xb, i] = term(xb, i).astype(BF16)
            cm[i] = send(
                x_out.at[xb, i], x_mid.at[i], cm_s.at[i], cm_r.at[i], x_dev[1 if i % 2 == 0 else 3]
            )
        for i in order:
            step = 3 if i % 2 == 0 else 1
            xb = (x + step) % NX
            x_out[xb, i] = term(xb, i).astype(BF16)
            send_x(step, i)
        for i in order:
            step = 1 if i % 2 == 0 else 3
            xb = (x + step) % NX
            part = term(xb, i)
            cm[i].wait_recv()
            x_out[xb, i] = (part + x_mid[i].astype(F32)).astype(BF16)
            send_x(step, i)
        for i in order:
            x_out[x, i] = term(x, i).astype(BF16)

    low = lax.broadcasted_iota(jnp.int32, (64, 128), 1) < 64

    def to_run(i):
        for side in range(2):
            cx[side, i].wait_recv()
        for h in range(2):
            cols = pl.ds(128 * h, 128)
            total = x_out[x, i, :, cols].astype(F32)
            for side in range(2):
                total = total + x_in[side, i, :, cols].astype(F32)
            turned = pltpu.roll(total, 64, 1)
            r_out[i, 2 * h] = jnp.where(low, total[:64], turned[64:]).astype(BF16)
            r_out[i, 2 * h + 1] = jnp.where(low, turned[:64], total[64:]).astype(BF16)
        for d in (1, 2, 3):
            cr[d, i] = send(
                r_out.at[i, (b + d) % NB], r_in.at[i, d - 1],
                cr_s.at[i, d - 1], cr_r.at[i, d - 1], r_dev[d],
            )

    def run_total(i):
        for d in (1, 2, 3):
            cr[d, i].wait_recv()
        total = r_out[i, b].astype(F32)
        for d in (1, 2, 3):
            total = total + r_in[i, d - 1].astype(F32)
        return total

    def to_strided(i):
        s_out[i - 1] = run_total(i).astype(BF16)
        cs[i] = send(s_out.at[i - 1], s_in.at[i - 1], cs_s.at[i - 1], cs_r.at[i - 1], s_dev[i])

    bu, be, by = {}, {}, {}
    factor = 1.0 / math.sqrt(16 * TOK)

    def tokens_to_core():
        for d in (1, 3, 2):
            tx[d].wait_recv()
        for yy in range(NY):
            bu[yy] = send(
                tok_in.at[2 * yy + 1 - c], tok_in_peer.at[yy], bu_s.at[yy], bu_r.at[yy], c_dev
            )

    def d_to_core(p):
        for k in (2 * p, 2 * p + 1):
            rows = pl.ds(*CHUNKS[k])
            bz[k].wait_recv()
            be[k] = send(d_in.at[rows], d_in_peer.at[rows], be_s.at[k], be_r.at[k], c_dev)

    def own_tokens():
        for k in range(NCH):
            bd[k].wait_recv()
        for yy in range(NY):
            bt[yy].wait_recv()

        def step(yy, _):
            own[yy] = dot(d_t[...], tok_cols(inner(yy, zh, c))) + dot(d_peer[...], tok_peer[yy])
            return 0

        lax.fori_loop(0, NY, step, 0)

    def to_y(k):
        at, n = CHUNKS[k]
        rows = pl.ds(at, n)
        be[k].wait_recv()
        for d in (1, 3, 2, 0):
            yy = (y + d) % NY
            total = (
                own[yy, rows, :]
                + dot(d_in[rows, :], tok_in[2 * yy + c])
                + dot(d_in_peer[rows, :], tok_in_peer[yy])
            )
            if d == 0:
                wg_ref[rows, :] = total
                continue
            y_out[d - 1, rows, :] = total.astype(BF16)
            by[d, k] = send(
                y_out.at[d - 1, rows], y_in.at[d - 1, rows],
                by_s.at[k, d - 1], by_r.at[k, d - 1], y_dev[d],
            )

    def finish(k):
        rows = pl.ds(*CHUNKS[k])
        total = wg_ref[rows, :]
        for d in (1, 3, 2):
            by[d, k].wait_recv()
            total = total + y_in[d - 1, rows, :].astype(F32)
        wg_ref[rows, :] = total * factor

    with jax.named_scope("gradients"):
        to_run(1)
        tokens_to_core()
        own_tokens()
        to_run(2)
        d_to_core(0)
        to_run(3)
        to_run(0)
        for yy in range(NY):
            bu[yy].wait_recv()
        to_y(0)
        to_strided(1)
        to_strided(2)
        to_y(1)
        d_to_core(1)
        to_strided(3)
        d_to_core(2)
        to_y(2)
        to_y(3)
        s_own[...] = run_total(0)
        for k in range(4, NCH):
            to_y(k)
        for k in range(NCH):
            finish(k)

    with jax.named_scope("token_grads_last"):
        for d in (1, 2, 3):
            cs[d].wait_recv()
        total = s_own[...]
        for i in (1, 2, 3):
            total = total + s_in[i - 1].astype(F32)
        tg_ref[:64, :] = total[:, :64]
        tg_ref[64:, :] = pltpu.roll(total, 64, 1)[:, :64]

    for copy in sent:
        copy.wait_send()


def local(tokens, weight_codes, block_scales, grad_hidden):
    units = weight_codes.shape[2]
    me = lax.axis_index("inner")
    block = me * COLS // BLOCK
    scales = lax.dynamic_index_in_dim(block_scales, block, 1, keepdims=True)
    weights = (weight_codes.astype(F32) * scales).astype(BF16)
    pad = HALF - units
    wt = jnp.pad(weights.transpose(0, 2, 1), ((0, 0), (0, pad), (0, 0))).reshape(ROWS, COLS)
    gh = jnp.pad(grad_hidden.T, ((0, pad), (0, 0)))
    dma = pltpu.SemaphoreType.DMA
    vmem = pl.BlockSpec(memory_space=pltpu.VMEM)
    hidden_t, token_grads, grads_t = pl.pallas_call(
        kernel,
        out_shape=(
            jax.ShapeDtypeStruct((HALF, TOK), BF16),
            jax.ShapeDtypeStruct((TOK, 64), F32),
            jax.ShapeDtypeStruct((ROWS, COLS), F32),
        ),
        in_specs=[vmem] * 3,
        out_specs=(vmem,) * 3,
        scratch_shapes=[
            pltpu.VMEM((16, ROWS, COLS), BF16),
            pltpu.VMEM((ROWS, COLS), BF16),
            pltpu.VMEM((16, COLS), BF16),
            pltpu.VMEM((ROWS, TOK), F32),
            pltpu.VMEM((ROWS, TOK), BF16),
            pltpu.VMEM((384, TOK), F32),
            pltpu.VMEM((TOK, 384), BF16),
            pltpu.VMEM((ROWS, TOK), BF16),
            pltpu.VMEM((2 * NY, TOK, COLS), BF16),
            pltpu.VMEM((NX, 4, TOK, COLS), BF16),
            pltpu.VMEM((4, TOK, COLS), BF16),
            pltpu.VMEM((2, 4, TOK, COLS), BF16),
            pltpu.VMEM((NA, NB, 64, 128), BF16),
            pltpu.VMEM((NA, NB - 1, 64, 128), BF16),
            pltpu.VMEM((64, 128), F32),
            pltpu.VMEM((NA - 1, 64, 128), BF16),
            pltpu.VMEM((NA - 1, 64, 128), BF16),
            pltpu.VMEM((NY, TOK, COLS), BF16),
            pltpu.VMEM((ROWS, TOK), BF16),
            pltpu.VMEM((NY, TOK, COLS), BF16),
            pltpu.VMEM((ROWS, TOK), BF16),
            pltpu.VMEM((NY, ROWS, COLS), F32),
            pltpu.VMEM((NY - 1, ROWS, COLS), BF16),
            pltpu.VMEM((NY - 1, ROWS, COLS), BF16),
            pltpu.SemaphoreType.REGULAR,
            dma((NCH,)), dma((NCH,)),
            dma((NCH,)), dma((NCH,)),
            dma((NY, 1 + NCH)), dma((NY, 1 + NCH)),
            dma((NY, 1 + NCH)), dma((NY, 1 + NCH)),
            dma((NCH,)), dma((NCH,)),
            dma((NY,)), dma((NY,)),
            dma((NCH,)), dma((NCH,)),
            dma((NY,)), dma((NY,)),
            dma((NCH,)), dma((NCH,)),
            dma((NCH, 3)), dma((NCH, 3)),
            dma((4,)), dma((4,)),
            dma((2, 4)), dma((2, 4)),
            dma((4, 3)), dma((4, 3)),
            dma((3,)), dma((3,)),
            dma((1,)), dma((1,)),
            dma((1,)), dma((1,)),
            dma((3,)), dma((3,)),
            dma((3,)), dma((3,)),
            dma((3,)), dma((3,)),
        ],
        compiler_params=pltpu.CompilerParams(
            collective_id=0, has_side_effects=True, vmem_limit_bytes=44 * 2**20
        ),
        name="ffn_grads",
    )(wt, tokens, gh)
    hidden = hidden_t[:units].T
    weight_grads = grads_t.reshape(2, HALF, COLS)[:, :units].transpose(0, 2, 1)
    return (hidden, token_grads, weight_grads)


def solution(mesh):
    return jax.shard_map(
        local,
        mesh=mesh,
        in_specs=(
            P("inner", None),
            P(None, "inner", "outer"),
            P(None, None, "outer"),
            P("inner", "outer"),
        ),
        out_specs=(P("inner", "outer"), P("inner", "outer"), P(None, "inner", "outer")),
        check_vma=False,
    )
```

```python
import math

import jax
import jax.numpy as jnp
from jax import lax
from jax.experimental import pallas as pl
from jax.experimental.pallas import tpu as pltpu
from jax.sharding import PartitionSpec as P

MESH = pl.DeviceIdType.MESH
BLOCK = 2048
F32 = jnp.float32
BF16 = jnp.bfloat16

NY, NX, NA, NB, NZ = 4, 4, 4, 4, 16
HALF = 176
ROWS = 2 * HALF
COLS = 256
TOK = 128
CHUNKS = ((0, 96), (176, 96), (96, 48), (272, 48), (144, 32), (320, 32))
NCH = len(CHUNKS)


def dot(a, b):
    return lax.dot_general(a, b, (((1,), (0,)), ((), ())), preferred_element_type=F32)


def dot_nt(a, b):
    return lax.dot_general(a, b, (((1,), (1,)), ((), ())), preferred_element_type=F32)


def kernel(
    wt_ref, tok_ref, gh_ref, hid_ref, tg_ref, wg_ref,
    w_all, w_mid, tok_mid, acc, d_t, d_f, d_b, d_in, tok_in,
    x_out, x_mid, x_in, r_out, r_in, s_own, s_out, s_in,
    tok_peer, d_peer, tok_in_peer, d_in_peer, own, y_out, y_in,
    near, f1_s, f1_r, fz_s, fz_r, fy_s, fy_r, fc_s, fc_r,
    bz_s, bz_r, bt_s, bt_r, bd_s, bd_r, bu_s, bu_r, be_s, be_r, by_s, by_r,
    cm_s, cm_r, cx_s, cx_r, cr_s, cr_r, cs_s, cs_r,
    tm_s, tm_r, ta_s, ta_r, ts_s, ts_r, tr_s, tr_r, tx_s, tx_r,
):
    me = lax.axis_index("inner")
    ou = lax.axis_index("outer")
    y, zh, c = me // 4, (me // 2) % 2, me % 2
    x, zl = ou // NZ, ou % NZ
    a, b = zl // NB, zl % NB

    def inner(yy, zz, cc):
        return yy * 4 + zz * 2 + cc

    z = zh * NZ + zl

    def along(hops):
        far = (z + hops) % (2 * NZ)
        return {"inner": inner(y, far // NZ, c), "outer": x * NZ + far % NZ}

    z_dev = {"inner": inner(y, 1 - zh, c)}
    leg = [along(8), along(24)]
    c_dev = {"inner": inner(y, zh, 1 - c)}
    y_dev = [{"inner": inner((y + d) % NY, zh, c)} for d in range(NY)]
    x_dev = [{"outer": ((x + d) % NX) * NZ + zl} for d in range(NX)]
    r_dev = [{"outer": x * NZ + a * NB + (b + d) % NB} for d in range(NB)]
    s_dev = [{"outer": x * NZ + ((a + d) % NA) * NB + b} for d in range(NA)]

    sent = []

    def send(src, dst, s_sem, r_sem, device):
        copy = pltpu.make_async_remote_copy(
            src_ref=src, dst_ref=dst, send_sem=s_sem, recv_sem=r_sem,
            device_id=device, device_id_type=MESH,
        )
        copy.start()
        sent.append(copy)
        return copy

    barrier = pltpu.get_barrier_semaphore()
    quarter = [along(4), along(28)]
    peers = leg + quarter + x_dev[1:] + y_dev[1:] + r_dev[1:] + [c_dev]
    for device in peers:
        pl.semaphore_signal(barrier, inc=1, device_id=device, device_id_type=MESH)
    w_all[me] = wt_ref[...]
    acc[...] = jnp.zeros_like(acc)
    pl.semaphore_wait(barrier, len(peers))
    for device in quarter:
        pl.semaphore_signal(near, inc=1, device_id=device, device_id_type=MESH)

    with jax.named_scope("gather_weights"):
        f1, fz, fy, fc = {}, {}, {}, {}
        shard = 2 * x + b // 2

        def shard_rows(aa):
            return pl.ds(pl.multiple_of((b % 2) * 64 + aa * 16, 16), 16)

        mine = shard_rows(a)
        shard_cols = inner(shard // 2, 1 - zh, shard % 2)
        shard_cols = pl.ds(pl.multiple_of(shard_cols * COLS, COLS), COLS)
        tok_leg = along(8 + 16 * c)
        tm = send(
            tok_ref.at[mine, shard_cols], tok_mid, tm_s.at[0], tm_r.at[0], tok_leg
        )
        for k, (at, n) in enumerate(CHUNKS):
            part = w_all.at[me, pl.ds(at, n)]
            f1[k] = send(part, w_mid.at[pl.ds(at, n)], f1_s.at[k], f1_r.at[k], leg[k % 2])
        block = w_all.at[me]
        for d in (1, 3, 2):
            fy[d, 0] = send(block, block, fy_s.at[d, 0], fy_r.at[d, 0], y_dev[d])
        fc[0, 0] = send(block, block, fc_s.at[0, 0], fc_r.at[0, 0], c_dev)

        def relay(k):
            at, n = CHUNKS[k]
            f1[k].wait_recv()
            origin = (z + (24 if k % 2 == 0 else 8)) % (2 * NZ) // NZ
            fz[k] = send(
                w_mid.at[pl.ds(at, n)], w_all.at[inner(y, origin, c), pl.ds(at, n)],
                fz_s.at[k], fz_r.at[k], leg[k % 2],
            )

        def tok_cols(j):
            return tok_ref[:, pl.ds(pl.multiple_of(j * COLS, COLS), COLS)]

        def add_blocks(side, at, n):
            total = acc[pl.ds(at, n), :]
            for t in range(2 * NY):
                j = inner(t // 2, side, t % 2)
                total = total + dot_nt(w_all[j, pl.ds(at, n), :], tok_cols(j))
            acc[pl.ds(at, n), :] = total

        def spread(k):
            at, n = CHUNKS[k]
            fz[k].wait_recv()
            part = w_all.at[inner(y, 1 - zh, c), pl.ds(at, n)]
            for d in (1, 3, 2):
                fy[d, 1 + k] = send(part, part, fy_s.at[d, 1 + k], fy_r.at[d, 1 + k], y_dev[d])
            fc[0, 1 + k] = send(part, part, fc_s.at[0, 1 + k], fc_r.at[0, 1 + k], c_dev)

        def pass_on(k):
            at, n = CHUNKS[k]
            for d in (1, 3, 2):
                fy[d, 1 + k].wait_recv()
                part = w_all.at[inner((y - d + NY) % NY, 1 - zh, c), pl.ds(at, n)]
                fc[d, 1 + k] = send(part, part, fc_s.at[d, 1 + k], fc_r.at[d, 1 + k], c_dev)

        def use(k):
            at, n = CHUNKS[k]
            for d in range(NY):
                fc[d, 1 + k].wait_recv()
            add_blocks(1 - zh, at, n)

        bt = {}
        for yy in range(NY):
            bt[yy] = send(
                tok_ref.at[:, pl.ds(pl.multiple_of(inner(yy, zh, 1 - c) * COLS, COLS), COLS)],
                tok_peer.at[yy], bt_s.at[yy], bt_r.at[yy], c_dev,
            )
        tm.wait_recv()
        ta = send(
            tok_mid, tok_in.at[shard, shard_rows((a + 2) % NA)], ta_s.at[0], ta_r.at[0], tok_leg
        )
        relay(0)
        relay(1)
        for d in (1, 3, 2):
            fy[d, 0].wait_recv()
            block = w_all.at[inner((y - d + NY) % NY, zh, c)]
            fc[d, 0] = send(block, block, fc_s.at[d, 0], fc_r.at[d, 0], c_dev)
        relay(2)
        relay(3)
        ta.wait_recv()
        pl.semaphore_wait(near, 2)
        ts = {}
        for d in (1, 2, 3):
            part = tok_in.at[shard, mine]
            ts[d] = send(part, part, ts_s.at[d - 1], ts_r.at[d - 1], s_dev[d])
        for d in range(NY):
            fc[d, 0].wait_recv()
        for at in range(0, ROWS, HALF):
            add_blocks(zh, at, HALF)
        spread(0)
        spread(1)
        relay(4)
        relay(5)
        pass_on(0)
        pass_on(1)
        spread(2)
        spread(3)
        tr, tx = {}, {}
        for d in (1, 2, 3):
            ts[d].wait_recv()
        run = tok_in.at[shard, pl.ds(pl.multiple_of((b % 2) * 64, 64), 64)]
        for d in (1, 2, 3):
            tr[d] = send(run, run, tr_s.at[d - 1], tr_r.at[d - 1], r_dev[d])

    bz, bd = {}, {}

    def activate(p):
        at, n = CHUNKS[2 * p]
        gate_rows, up_rows = pl.ds(at, n), pl.ds(HALF + at, n)
        gate = acc[gate_rows, :]
        up = acc[up_rows, :]
        sig = jax.nn.sigmoid(gate)
        silu = gate * sig
        hid_ref[gate_rows, :] = (silu * up).astype(BF16)
        cot = gh_ref[gate_rows, :].astype(F32)
        d_gate = (cot * up * sig * (1.0 + gate * (1.0 - sig))).astype(BF16)
        d_up = (cot * silu).astype(BF16)
        d_t[gate_rows, :] = d_gate
        d_t[up_rows, :] = d_up
        d_f[gate_rows, :] = d_gate.astype(F32)
        d_f[up_rows, :] = d_up.astype(F32)

    def send_d(p):
        for k in (2 * p, 2 * p + 1):
            rows = pl.ds(*CHUNKS[k])
            bz[k] = send(d_t.at[rows], d_in.at[rows], bz_s.at[k], bz_r.at[k], z_dev)
            bd[k] = send(d_t.at[rows], d_peer.at[rows], bd_s.at[k], bd_r.at[k], c_dev)

    with jax.named_scope("activations"):
        use(0)
        use(1)
        pass_on(2)
        pass_on(3)
        activate(0)
        spread(4)
        spread(5)
        send_d(0)
        use(2)
        use(3)
        pass_on(4)
        pass_on(5)
        activate(1)
        send_d(1)
        for d in (1, 2, 3):
            tr[d].wait_recv()
        pair = tok_in.at[pl.ds(2 * x, 2)]
        for d in (1, 3, 2):
            tx[d] = send(pair, pair, tx_s.at[d - 1], tx_r.at[d - 1], x_dev[d])
        use(4)
        use(5)
        activate(2)
        send_d(2)
        d_f[ROWS:, :] = jnp.zeros((d_f.shape[0] - ROWS, TOK), F32)
        d_b[...] = d_f[...].T.astype(BF16)

    cm, cx, cr, cs = {}, {}, {}, {}
    order = (1, 2, 3, 0)
    quarters = [(a + i) % NA for i in range(NA)]

    def term(xb, i):
        return dot(d_b[:, :ROWS], w_all[4 * xb + quarters[i]])

    def send_x(step, i):
        side = 0 if step == 1 else 1
        cx[side, i] = send(
            x_out.at[(x + step) % NX, i], x_in.at[side, i],
            cx_s.at[side, i], cx_r.at[side, i], x_dev[step],
        )

    with jax.named_scope("token_grads_x"):
        for i in order:
            xb = (x + 2) % NX
            x_out[xb, i] = term(xb, i).astype(BF16)
            cm[i] = send(
                x_out.at[xb, i], x_mid.at[i], cm_s.at[i], cm_r.at[i], x_dev[1 if i % 2 == 0 else 3]
            )
        for i in order:
            step = 3 if i % 2 == 0 else 1
            xb = (x + step) % NX
            x_out[xb, i] = term(xb, i).astype(BF16)
            send_x(step, i)
        for i in order:
            step = 1 if i % 2 == 0 else 3
            xb = (x + step) % NX
            part = term(xb, i)
            cm[i].wait_recv()
            x_out[xb, i] = (part + x_mid[i].astype(F32)).astype(BF16)
            send_x(step, i)
        for i in order:
            x_out[x, i] = term(x, i).astype(BF16)

    low = lax.broadcasted_iota(jnp.int32, (64, 128), 1) < 64

    def to_run(i):
        for side in range(2):
            cx[side, i].wait_recv()
        for h in range(2):
            cols = pl.ds(128 * h, 128)
            total = x_out[x, i, :, cols].astype(F32)
            for side in range(2):
                total = total + x_in[side, i, :, cols].astype(F32)
            turned = pltpu.roll(total, 64, 1)
            r_out[i, 2 * h] = jnp.where(low, total[:64], turned[64:]).astype(BF16)
            r_out[i, 2 * h + 1] = jnp.where(low, turned[:64], total[64:]).astype(BF16)
        for d in (1, 2, 3):
            cr[d, i] = send(
                r_out.at[i, (b + d) % NB], r_in.at[i, d - 1],
                cr_s.at[i, d - 1], cr_r.at[i, d - 1], r_dev[d],
            )

    def run_total(i):
        for d in (1, 2, 3):
            cr[d, i].wait_recv()
        total = r_out[i, b].astype(F32)
        for d in (1, 2, 3):
            total = total + r_in[i, d - 1].astype(F32)
        return total

    def to_strided(i):
        s_out[i - 1] = run_total(i).astype(BF16)
        cs[i] = send(s_out.at[i - 1], s_in.at[i - 1], cs_s.at[i - 1], cs_r.at[i - 1], s_dev[i])

    bu, be, by = {}, {}, {}
    factor = 1.0 / math.sqrt(16 * TOK)

    def tokens_to_core():
        for d in (1, 3, 2):
            tx[d].wait_recv()
        for yy in range(NY):
            bu[yy] = send(
                tok_in.at[2 * yy + 1 - c], tok_in_peer.at[yy], bu_s.at[yy], bu_r.at[yy], c_dev
            )

    def d_to_core(p):
        for k in (2 * p, 2 * p + 1):
            rows = pl.ds(*CHUNKS[k])
            bz[k].wait_recv()
            be[k] = send(d_in.at[rows], d_in_peer.at[rows], be_s.at[k], be_r.at[k], c_dev)

    def own_tokens():
        for k in range(NCH):
            bd[k].wait_recv()
        for yy in range(NY):
            bt[yy].wait_recv()

        def step(yy, _):
            own[yy] = dot(d_t[...], tok_cols(inner(yy, zh, c))) + dot(d_peer[...], tok_peer[yy])
            return 0

        lax.fori_loop(0, NY, step, 0)

    def to_y(k):
        at, n = CHUNKS[k]
        rows = pl.ds(at, n)
        be[k].wait_recv()
        for d in (1, 3, 2, 0):
            yy = (y + d) % NY
            total = (
                own[yy, rows, :]
                + dot(d_in[rows, :], tok_in[2 * yy + c])
                + dot(d_in_peer[rows, :], tok_in_peer[yy])
            )
            if d == 0:
                wg_ref[rows, :] = total
                continue
            y_out[d - 1, rows, :] = total.astype(BF16)
            by[d, k] = send(
                y_out.at[d - 1, rows], y_in.at[d - 1, rows],
                by_s.at[k, d - 1], by_r.at[k, d - 1], y_dev[d],
            )

    def finish(k):
        rows = pl.ds(*CHUNKS[k])
        total = wg_ref[rows, :]
        for d in (1, 3, 2):
            by[d, k].wait_recv()
            total = total + y_in[d - 1, rows, :].astype(F32)
        wg_ref[rows, :] = total * factor

    with jax.named_scope("gradients"):
        tokens_to_core()
        d_to_core(0)
        to_run(1)
        own_tokens()
        to_run(2)
        d_to_core(1)
        to_run(3)
        to_run(0)
        for yy in range(NY):
            bu[yy].wait_recv()
        to_y(0)
        to_y(1)
        to_strided(1)
        to_strided(2)
        to_y(2)
        to_y(3)
        to_strided(3)
        d_to_core(2)
        s_own[...] = run_total(0)
        for k in range(4, NCH):
            to_y(k)
        for k in range(NCH):
            finish(k)

    with jax.named_scope("token_grads_last"):
        for d in (1, 2, 3):
            cs[d].wait_recv()
        total = s_own[...]
        for i in (1, 2, 3):
            total = total + s_in[i - 1].astype(F32)
        tg_ref[:64, :] = total[:, :64]
        tg_ref[64:, :] = pltpu.roll(total, 64, 1)[:, :64]

    for copy in sent:
        copy.wait_send()


def local(tokens, weight_codes, block_scales, grad_hidden):
    units = weight_codes.shape[2]
    me = lax.axis_index("inner")
    block = me * COLS // BLOCK
    scales = lax.dynamic_index_in_dim(block_scales, block, 1, keepdims=True)
    weights = (weight_codes.astype(F32) * scales).astype(BF16)
    pad = HALF - units
    wt = jnp.pad(weights.transpose(0, 2, 1), ((0, 0), (0, pad), (0, 0))).reshape(ROWS, COLS)
    gh = jnp.pad(grad_hidden.T, ((0, pad), (0, 0)))
    dma = pltpu.SemaphoreType.DMA
    vmem = pl.BlockSpec(memory_space=pltpu.VMEM)
    hidden_t, token_grads, grads_t = pl.pallas_call(
        kernel,
        out_shape=(
            jax.ShapeDtypeStruct((HALF, TOK), BF16),
            jax.ShapeDtypeStruct((TOK, 64), F32),
            jax.ShapeDtypeStruct((ROWS, COLS), F32),
        ),
        in_specs=[vmem] * 3,
        out_specs=(vmem,) * 3,
        scratch_shapes=[
            pltpu.VMEM((16, ROWS, COLS), BF16),
            pltpu.VMEM((ROWS, COLS), BF16),
            pltpu.VMEM((16, COLS), BF16),
            pltpu.VMEM((ROWS, TOK), F32),
            pltpu.VMEM((ROWS, TOK), BF16),
            pltpu.VMEM((384, TOK), F32),
            pltpu.VMEM((TOK, 384), BF16),
            pltpu.VMEM((ROWS, TOK), BF16),
            pltpu.VMEM((2 * NY, TOK, COLS), BF16),
            pltpu.VMEM((NX, 4, TOK, COLS), BF16),
            pltpu.VMEM((4, TOK, COLS), BF16),
            pltpu.VMEM((2, 4, TOK, COLS), BF16),
            pltpu.VMEM((NA, NB, 64, 128), BF16),
            pltpu.VMEM((NA, NB - 1, 64, 128), BF16),
            pltpu.VMEM((64, 128), F32),
            pltpu.VMEM((NA - 1, 64, 128), BF16),
            pltpu.VMEM((NA - 1, 64, 128), BF16),
            pltpu.VMEM((NY, TOK, COLS), BF16),
            pltpu.VMEM((ROWS, TOK), BF16),
            pltpu.VMEM((NY, TOK, COLS), BF16),
            pltpu.VMEM((ROWS, TOK), BF16),
            pltpu.VMEM((NY, ROWS, COLS), F32),
            pltpu.VMEM((NY - 1, ROWS, COLS), BF16),
            pltpu.VMEM((NY - 1, ROWS, COLS), BF16),
            pltpu.SemaphoreType.REGULAR,
            dma((NCH,)), dma((NCH,)),
            dma((NCH,)), dma((NCH,)),
            dma((NY, 1 + NCH)), dma((NY, 1 + NCH)),
            dma((NY, 1 + NCH)), dma((NY, 1 + NCH)),
            dma((NCH,)), dma((NCH,)),
            dma((NY,)), dma((NY,)),
            dma((NCH,)), dma((NCH,)),
            dma((NY,)), dma((NY,)),
            dma((NCH,)), dma((NCH,)),
            dma((NCH, 3)), dma((NCH, 3)),
            dma((4,)), dma((4,)),
            dma((2, 4)), dma((2, 4)),
            dma((4, 3)), dma((4, 3)),
            dma((3,)), dma((3,)),
            dma((1,)), dma((1,)),
            dma((1,)), dma((1,)),
            dma((3,)), dma((3,)),
            dma((3,)), dma((3,)),
            dma((3,)), dma((3,)),
        ],
        compiler_params=pltpu.CompilerParams(
            collective_id=0, has_side_effects=True, vmem_limit_bytes=44 * 2**20
        ),
        name="ffn_grads",
    )(wt, tokens, gh)
    hidden = hidden_t[:units].T
    weight_grads = grads_t.reshape(2, HALF, COLS)[:, :units].transpose(0, 2, 1)
    return (hidden, token_grads, weight_grads)


def solution(mesh):
    return jax.shard_map(
        local,
        mesh=mesh,
        in_specs=(
            P("inner", None),
            P(None, "inner", "outer"),
            P(None, None, "outer"),
            P("inner", "outer"),
        ),
        out_specs=(P("inner", "outer"), P("inner", "outer"), P(None, "inner", "outer")),
        check_vma=False,
    )
```
